32 devices in a mesh: gx: 4 (over z), gy: 8 (over y, x, core).
Axes of the slice: x: 2, y: 2, z: 4, core: 2. Of those that a mesh axis runs over, the one named last changes fastest.
Arguments:
- a_tiles: float32 [256, 4, 128, 128], P(('gx', 'gy')), may hold values from -6 to 6
- a_cols: int32 [256, 4], P(('gx', 'gy')), may hold values from 0 to 255, as said below
- new_row: int32 [256], P(('gx', 'gy')), may hold values from 0 to 255, as said below
- p_tiles: float32 [256, 2, 128, 128], P(('gx', 'gy')), may hold values from -0.5 to 0.5
- p_cols: int32 [256, 2], P(('gx', 'gy')), may hold values from 0 to 63, as said below
Outputs:
- coarse: float32 [64, 10, 128, 128], P(('gx', 'gy'))
The draws below stay inside these ranges and needn't reach their ends.
Inputs may be any that keep to these rules, and one draw needn't show every extreme that they name: A permutation; the new owner new_row // 8 of a block row has the same gy index as its old owner and a gx index 0 to 3 above the old owner's, modulo the number of gx indices; at most 2 block rows of one device go to one new owner. `a_cols`: the first column block of old block row o is new_row[o]; the others are distinct block rows of the devices with the same gx index as new_row[o]'s owner and gy index one below, equal or one above. `p_cols`: for block row g owned by device d (gy index y), the first coarse block is one of d's 2 coarse blocks, the second one of device d + 1's, or of d's where y is the last gy index.
All inputs are finite; a program needn't handle non-finite values.
Results may differ from the reference program's by a relative error of at most 0.0003.
Values sent between devices are 32-bit elements; how exact they have to be, the bound alone decides.
A program may use at most 128 MiB of HBM per device.

```python
import jax
import jax.numpy as jnp
from jax import lax

TILE = 128
ROWS_DEV = 8
GROUPS = 4
A_TILES = 4
P_TILES = 2
SPAN = 4
CAP = 2
COARSE_DEV = 2
SLOTS = 10
NB = 256
NC = 64
N_GX = 4
N_GY = 8


def migration(key):
    first_key, second_key = jax.random.split(jax.random.fold_in(key, 11))
    scores = jax.random.randint(first_key, (N_GY, SPAN), 0, 1 << 20) * 64 + jnp.arange(SPAN)[None, :]
    offsets = jnp.argsort(scores, axis=1)[:, :GROUPS]
    slot_scores = jax.random.randint(second_key, (N_GX, N_GY, ROWS_DEV), 0, 1 << 20) * 256 + jnp.arange(ROWS_DEV)[None, None, :]
    position = jnp.argsort(slot_scores, axis=2).astype(jnp.int32)
    group_id = position // CAP
    within = position % CAP
    column_y = jnp.broadcast_to(jnp.arange(N_GY)[None, :, None], position.shape)
    source_x = jnp.broadcast_to(jnp.arange(N_GX)[:, None, None], position.shape)
    target_x = (source_x + offsets[column_y, group_id]) % N_GX
    result = (target_x * N_GY + column_y) * ROWS_DEV + group_id * CAP + within
    return result.reshape(-1).astype(jnp.int32)


def draw_new_row(key, part):
    return migration(key)


def draw_a_cols(key, part):
    moved_to = migration(key)
    pick_key = jax.random.fold_in(key, 23)
    total = ROWS_DEV * N_GX * N_GY
    block_row = jnp.arange(total)
    device_id = block_row // ROWS_DEV
    column_y = device_id % N_GY
    window = jnp.arange(3 * ROWS_DEV)
    cand_y = column_y[:, None] - 1 + window[None, :] // ROWS_DEV
    candidate = (device_id[:, None] - 1 + window[None, :] // ROWS_DEV) * ROWS_DEV + window[None, :] % ROWS_DEV
    usable = (cand_y >= 0) & (cand_y < N_GY) & (candidate != block_row[:, None])
    scores = jax.random.randint(pick_key, (total, 3 * ROWS_DEV), 0, 1 << 20) * 512 + window[None, :]
    scores = jnp.where(usable, scores, 1 << 30)
    order_index = jnp.argsort(scores, axis=1)[:, :A_TILES - 1]
    chosen = jnp.take_along_axis(candidate, order_index, axis=1)
    columns_new = jnp.concatenate([block_row[:, None], chosen], axis=1).astype(jnp.int32)
    return columns_new[moved_to]


def draw_p_cols(key, part):
    first_key, second_key = jax.random.split(jax.random.fold_in(key, 37))
    total = ROWS_DEV * N_GX * N_GY
    device_id = jnp.arange(total) // ROWS_DEV
    column_y = device_id % N_GY
    first_block = jax.random.randint(first_key, (total,), 0, COARSE_DEV)
    second_block = jax.random.randint(second_key, (total,), 0, COARSE_DEV)
    next_device = jnp.where(column_y < N_GY - 1, device_id + 1, device_id)
    return jnp.stack([device_id * COARSE_DEV + first_block, next_device * COARSE_DEV + second_block], axis=1).astype(jnp.int32)


def levels(own_key, dims, pieces, low, largest):
    factor_of = 1.0
    for dim, parts in pieces:
        steps = jax.random.uniform(jax.random.fold_in(jax.random.fold_in(own_key, 6), dim), (parts,), jnp.float32, low / len(pieces), largest / len(pieces))
        factor_of = factor_of * jnp.repeat(jnp.exp(steps), dims[dim] // parts).reshape((-1,) + (1,) * (len(dims) - 1 - dim))
    return factor_of


def normal_values(own_key, shape, width, limit, shards=(), dtype=jnp.bfloat16):
    level = levels(own_key, shape, shards, -0.22, 0.18) if shards else 1.0
    array = jax.random.normal(own_key, shape, jnp.float32) * width * level
    return jnp.minimum(jnp.maximum(array, -limit), limit).astype(dtype)


def setup_inputs(seed: int = 0) -> dict:
    splits = jax.random.split(jax.random.key(seed), 6)
    a_tiles = normal_values(splits[0], (NB, A_TILES, TILE, TILE), 1.0, 6.0, ((0, 32),), jnp.float32)
    a_cols = draw_a_cols(jax.random.fold_in(splits[5], 71), 0)
    new_row = draw_new_row(jax.random.fold_in(splits[5], 71), 0)
    p_tiles = normal_values(splits[3], (NB, P_TILES, TILE, TILE), TILE ** -0.5, 0.5, ((0, 32),), jnp.float32)
    p_cols = draw_p_cols(jax.random.fold_in(splits[5], 71), 0)
    return {"a_tiles": a_tiles, "a_cols": a_cols, "new_row": new_row, "p_tiles": p_tiles, "p_cols": p_cols}


def reference(a_tiles, a_cols, new_row, p_tiles, p_cols):
    moved = jnp.zeros_like(a_tiles).at[new_row].set(a_tiles)
    moved_cols = jnp.zeros_like(a_cols).at[new_row].set(a_cols)
    coarse = jnp.zeros((NC, SLOTS, TILE, TILE), jnp.float32)

    def add_row(total, row_data):
        tiles, columns, own_tiles, own_cols = row_data
        fetched = p_tiles[columns]
        products = jnp.einsum("kab,kqbc->kqac", tiles, fetched, precision=lax.Precision.HIGHEST)
        targets = p_cols[columns]
        terms = jnp.einsum("pba,kqbc->pkqac", own_tiles, products, precision=lax.Precision.HIGHEST)
        relative = targets[None, :, :] // COARSE_DEV - own_cols[:, None, None] // COARSE_DEV + 2
        slot_index = relative * COARSE_DEV + targets[None, :, :] % COARSE_DEV
        row_index = jnp.broadcast_to(own_cols[:, None, None], slot_index.shape)
        total = total.at[row_index.reshape(-1), slot_index.reshape(-1)].add(terms.reshape(-1, TILE, TILE))
        return total, None

    coarse, unused = lax.scan(add_row, coarse, (moved, moved_cols, p_tiles, p_cols))
    return coarse
```

```python
import functools

import jax
import jax.numpy as jnp
from jax import lax
from jax.experimental import pallas as pl
from jax.experimental.pallas import tpu as pltpu
from jax.sharding import PartitionSpec as P

A_TILES = 4
P_TILES = 2
CAP = 2
SPAN = 6
LANES = 128
ROW_LANE = A_TILES
P_LANE = A_TILES + 1


def split(value):
    high = value.astype(jnp.bfloat16)
    low = (value - high.astype(jnp.float32)).astype(jnp.bfloat16)
    return high, low


def find_row(new_row_of, rows, per_owner, owner, rank):
    seen = jnp.int32(0)
    found = jnp.int32(0)
    for row in range(rows):
        here = lax.div(new_row_of(row), jnp.int32(per_owner)) == owner
        found = jnp.where(here & (seen == rank), row, found)
        seen = seen + here.astype(jnp.int32)
    return found, seen > rank


def kernel(
    span, gx, gy,
    new_row_ref, a_cols_ref, p_cols_ref, a_ref, p_ref,
    own_ref, arrived_ref,
    stage, recv, ext, ext_cat, flipped, products, following,
    table, table_from, table_ext, from_s, ext_s,
    a_send, a_recv, t_send, t_recv, h_send, h_recv, ht_send, ht_recv, n_send, n_recv, local_sem,
):
    rows, tile = p_ref.shape[0], p_ref.shape[2]
    coarse = rows // 4
    chunks = 4 * coarse // 2
    x, y = lax.axis_index("gx"), lax.axis_index("gy")
    device = x * gy + y
    per_owner = rows * gy
    has_left, has_right = y > 0, y < gy - 1

    barrier = pltpu.get_barrier_semaphore()
    for step in range(1, span):
        pl.semaphore_signal(
            barrier, inc=1, device_id={"gx": lax.rem(x + gx - step, gx)},
            device_id_type=pl.DeviceIdType.MESH)

    @pl.when(has_left)
    def _():
        pl.semaphore_signal(
            barrier, inc=1, device_id={"gy": y - 1}, device_id_type=pl.DeviceIdType.MESH)

    @pl.when(has_right)
    def _():
        pl.semaphore_signal(
            barrier, inc=1, device_id={"gy": y + 1}, device_id_type=pl.DeviceIdType.MESH)

    row_id = lax.broadcasted_iota(jnp.int32, (rows, LANES), 0)
    lane_id = lax.broadcasted_iota(jnp.int32, (rows, LANES), 1)
    filled = jnp.zeros((rows, LANES), jnp.int32)
    for row in range(rows):
        entries = [a_cols_ref[row, k] for k in range(A_TILES)]
        entries += [new_row_ref[row]]
        entries += [p_cols_ref[row, q] for q in range(P_TILES)]
        for lane, entry in enumerate(entries):
            filled = jnp.where((row_id == row) & (lane_id == lane), entry, filled)
    table[...] = filled
    table_from[0] = filled
    table_ext[1] = filled

    def put_rows(step, target, slot):
        owner = lax.rem(x + step, gx)
        for rank in range(CAP):
            row, _ = find_row(lambda r: new_row_ref[r], rows, per_owner, owner, rank)
            target[slot, rank] = a_ref[row]

    def a_copy(step):
        return pltpu.make_async_remote_copy(
            stage.at[step], recv.at[step], a_send.at[step], a_recv.at[step],
            device_id={"gx": lax.rem(x + step, gx)}, device_id_type=pl.DeviceIdType.MESH)

    def table_copy(step):
        return pltpu.make_async_remote_copy(
            table, table_from.at[step], t_send.at[step], t_recv.at[step],
            device_id={"gx": lax.rem(x + step, gx)}, device_id_type=pl.DeviceIdType.MESH)

    def halo_copies(side):
        target = y + 1 if side == 0 else y - 1
        place = 0 if side == 0 else 2
        return (
            pltpu.make_async_remote_copy(
                table, table_ext.at[place], ht_send.at[side], ht_recv.at[side],
                device_id={"gy": target}, device_id_type=pl.DeviceIdType.MESH),
            pltpu.make_async_remote_copy(
                p_ref, ext.at[side], h_send.at[side], h_recv.at[side],
                device_id={"gy": target}, device_id_type=pl.DeviceIdType.MESH),
        )

    if gx == 4 and span == 4:
        odd = lax.rem(x, 2)
        send_order = [2, 3 - 2 * odd, 1 + 2 * odd]

        def arrival(n):
            later = n // 2
            return 2 * n * (1 - later) + later * (
                (1 - odd) * (1 + 2 * (n - 2)) + odd * (3 - 2 * (n - 2)))
    else:
        send_order = list(range(1, span))

        def arrival(n):
            return n

    put_rows(send_order[0], stage, send_order[0])
    greeted = span - 1 + jnp.where(has_left, 1, 0) + jnp.where(has_right, 1, 0)
    pl.semaphore_wait(barrier, greeted)
    a_copy(send_order[0]).start()
    for step in range(1, span):
        table_copy(step).start()

    @pl.when(has_right)
    def _():
        for copy in halo_copies(0):
            copy.start()

    @pl.when(has_left)
    def _():
        for copy in halo_copies(1):
            copy.start()

    for step in send_order[1:]:
        put_rows(step, stage, step)
        a_copy(step).start()
    put_rows(0, recv, 0)

    def split_p(source, base):
        def body(row, carry):
            for q in range(P_TILES):
                high, low = split(source[row, q])
                columns = pl.ds(q * tile, tile)
                ext_cat[base + row, pl.ds(0, tile), columns] = high
                ext_cat[base + row, pl.ds(tile, tile), columns] = high
                ext_cat[base + row, pl.ds(2 * tile, tile), columns] = low
            return carry
        lax.fori_loop(0, rows, body, 0)

    def flip(row, carry):
        for q in range(P_TILES):
            flipped[row, q] = p_ref[row, q].T
        return carry

    lax.fori_loop(0, rows, flip, 0)
    split_p(p_ref, rows)

    def clear(n, carry):
        for t in range(coarse):
            own_ref[t, n] = jnp.zeros((tile, tile), jnp.float32)
            following[t, n] = jnp.zeros((tile, tile), jnp.float32)
        return carry

    lax.fori_loop(0, 4 * coarse, clear, 0)

    for step in range(1, span):
        table_copy(step).wait_recv()

    @pl.when(has_left)
    def _():
        for copy in halo_copies(0):
            copy.wait_recv()
        split_p(ext.at[0], 0)

    @pl.when(jnp.logical_not(has_left))
    def _():
        table_ext[0] = jnp.zeros((rows, LANES), jnp.int32)

    @pl.when(has_right)
    def _():
        for copy in halo_copies(1):
            copy.wait_recv()
        split_p(ext.at[1], 2 * rows)

    @pl.when(jnp.logical_not(has_right))
    def _():
        table_ext[2] = jnp.zeros((rows, LANES), jnp.int32)

    to_scalar = (
        pltpu.make_async_copy(table_from, from_s, local_sem.at[0]),
        pltpu.make_async_copy(table_ext, ext_s, local_sem.at[1]),
    )
    for copy in to_scalar:
        copy.start()
    for copy in to_scalar:
        copy.wait()

    def next_copy(n):
        piece = pl.ds(2 * n, 2)
        return pltpu.make_async_remote_copy(
            following.at[:, piece], arrived_ref.at[:, piece], n_send.at[n], n_recv.at[n],
            device_id={"gy": y + 1}, device_id_type=pl.DeviceIdType.MESH)

    def one_distance(n, carry):
        step = arrival(n)

        @pl.when(n > 0)
        def _():
            a_copy(step).wait_recv()

        slots = []
        lifts = [[] for _ in range(2 * coarse)]
        for rank in range(CAP):
            row, there = find_row(
                lambda r: from_s[step, r, ROW_LANE], rows, per_owner, x, rank)
            own_row = lax.rem(from_s[step, row, ROW_LANE], jnp.int32(rows))
            wide = []
            for k in range(A_TILES):
                column = jnp.where(there, from_s[step, row, k] - (device - 1) * rows, rows)
                column = jnp.minimum(jnp.maximum(column, 0), 3 * rows - 1)
                for q in range(P_TILES):
                    goal = ext_s[lax.div(column, rows), lax.rem(column, rows), P_LANE + q]
                    wide.append(jnp.where(there, goal - (device - 1) * coarse, -1))
                high, low = split(recv[step, rank, k])
                left = jnp.concatenate([high, low, high], axis=1)
                products[rank, k] = jnp.dot(
                    left, ext_cat[column], preferred_element_type=jnp.float32)
            slots.append(wide)
            goals = [
                ext_s[1, own_row, P_LANE + p] - device * coarse for p in range(P_TILES)]
            for t in range(2 * coarse):
                lifts[t].append(sum(
                    jnp.where(goals[p] == t, 1.0, 0.0) * flipped[own_row, p]
                    for p in range(P_TILES)))
        lift_cat = []
        for t in range(2 * coarse):
            high, low = split(jnp.concatenate(lifts[t], axis=1))
            lift_cat.append(jnp.concatenate([high, low, high], axis=1))
        lift_cat = jnp.concatenate(lift_cat, axis=0)

        def one_chunk(c, carry):
            halves = []
            for q in range(2):
                w = 2 * c + q
                parts = []
                for rank in range(CAP):
                    total = None
                    for m in range(A_TILES * P_TILES):
                        k, p = m // P_TILES, m % P_TILES
                        weight = jnp.where(slots[rank][m] == w, 1.0, 0.0)
                        term = weight * products[rank, k, :, pl.ds(p * tile, tile)]
                        total = term if total is None else total + term
                    parts.append(total)
                high, low = split(jnp.concatenate(parts, axis=0))
                halves.append(jnp.concatenate([high, high, low], axis=0))
            right = jnp.concatenate(halves, axis=1)
            result = jnp.dot(lift_cat, right, preferred_element_type=jnp.float32)
            for t in range(2 * coarse):
                for q in range(2):
                    value = result[t * tile:(t + 1) * tile, q * tile:(q + 1) * tile]
                    if t < coarse:
                        own_ref[t, 2 * c + q] += value
                    else:
                        following[t - coarse, 2 * c + q] += value

            @pl.when((n == span - 1) & has_right)
            def _():
                next_copy(c).start()

            return carry

        lax.fori_loop(0, chunks, one_chunk, 0)
        return carry

    lax.fori_loop(0, span, one_distance, 0)

    for step in range(1, span):
        table_copy(step).wait_send()
        a_copy(step).wait_send()

    @pl.when(has_right)
    def _():
        for copy in halo_copies(0):
            copy.wait_send()
        for c in range(chunks):
            next_copy(c).wait_send()

    @pl.when(has_left)
    def _():
        for copy in halo_copies(1):
            copy.wait_send()
        for c in range(chunks):
            next_copy(c).wait_recv()


def shards(a_tiles, a_cols, new_row, p_tiles, p_cols):
    rows, tile = a_tiles.shape[0], a_tiles.shape[2]
    gx, gy = lax.axis_size("gx"), lax.axis_size("gy")
    span = min(SPAN, gx)
    coarse = rows // 4
    vmem = pl.BlockSpec(memory_space=pltpu.VMEM)
    smem = pl.BlockSpec(memory_space=pltpu.SMEM)
    band = jax.ShapeDtypeStruct((coarse, 4 * coarse, tile, tile), jnp.float32)
    dma = pltpu.SemaphoreType.DMA
    row_block = (span, CAP, A_TILES, tile, tile)
    own, arrived = pl.pallas_call(
        functools.partial(kernel, span, gx, gy),
        out_shape=(band, band),
        in_specs=[smem, smem, smem, vmem, vmem],
        out_specs=(vmem, pl.BlockSpec(memory_space=pl.ANY)),
        scratch_shapes=[
            pltpu.VMEM(row_block, jnp.float32),
            pltpu.VMEM(row_block, jnp.float32),
            pltpu.VMEM((2, rows, P_TILES, tile, tile), jnp.float32),
            pltpu.VMEM((3 * rows, 3 * tile, P_TILES * tile), jnp.bfloat16),
            pltpu.VMEM((rows, P_TILES, tile, tile), jnp.float32),
            pltpu.VMEM((CAP, A_TILES, tile, P_TILES * tile), jnp.float32),
            pltpu.VMEM((coarse, 4 * coarse, tile, tile), jnp.float32),
            pltpu.VMEM((rows, LANES), jnp.int32),
            pltpu.VMEM((span, rows, LANES), jnp.int32),
            pltpu.VMEM((3, rows, LANES), jnp.int32),
            pltpu.SMEM((span, rows, LANES), jnp.int32),
            pltpu.SMEM((3, rows, LANES), jnp.int32),
            dma((span,)), dma((span,)), dma((span,)), dma((span,)),
            dma((2,)), dma((2,)), dma((2,)), dma((2,)),
            dma((2 * coarse,)), dma((2 * coarse,)), dma((2,)),
        ],
        compiler_params=pltpu.CompilerParams(
            collective_id=0, has_side_effects=True, vmem_limit_bytes=48 * 1024 * 1024),
        name="galerkin",
    )(new_row, a_cols, p_cols, a_tiles, p_tiles)
    arrived = jnp.where(lax.axis_index("gy") > 0, arrived, 0.0)
    pad = ((0, 0), (coarse, 0), (0, 0), (0, 0))
    behind = ((0, 0), (0, coarse), (0, 0), (0, 0))
    return jnp.pad(own, pad) + jnp.pad(arrived, behind)


def solution(mesh):
    in_specs = (
        P(("gx", "gy"), None, None, None),
        P(("gx", "gy"), None),
        P(("gx", "gy")),
        P(("gx", "gy"), None, None, None),
        P(("gx", "gy"), None),
    )
    out_specs = P(("gx", "gy"), None, None, None)
    return jax.shard_map(shards, mesh=mesh, in_specs=in_specs, out_specs=out_specs, check_vma=False)
```

```python
import functools

import jax
import jax.numpy as jnp
from jax import lax
from jax.experimental import pallas as pl
from jax.experimental.pallas import tpu as pltpu
from jax.sharding import PartitionSpec as P

A_TILES = 4
P_TILES = 2
CAP = 2
SPAN = 6
LANES = 128
ROW_LANE = A_TILES
P_LANE = A_TILES + 1


def split(value):
    high = value.astype(jnp.bfloat16)
    low = (value - high.astype(jnp.float32)).astype(jnp.bfloat16)
    return high, low


def find_row(new_row_of, rows, per_owner, owner, rank):
    seen = jnp.int32(0)
    found = jnp.int32(0)
    for row in range(rows):
        here = lax.div(new_row_of(row), jnp.int32(per_owner)) == owner
        found = jnp.where(here & (seen == rank), row, found)
        seen = seen + here.astype(jnp.int32)
    return found, seen > rank


def kernel(
    span, gx, gy,
    new_row_hbm, a_cols_hbm, p_cols_hbm, a_hbm, p_hbm,
    own_out, arrived_ref,
    own_ref, new_row_ref, a_cols_ref, p_cols_ref, a_ref, p_ref,
    stage, recv, ext, ext_cat, flipped, products, following,
    table, table_from, table_ext, from_s, ext_s,
    a_send, a_recv, t_send, t_recv, h_send, h_recv, ht_send, ht_recv, n_send, n_recv, local_sem, gate, o_sem,
):
    rows, tile = p_ref.shape[0], p_ref.shape[2]
    coarse = rows // 4
    chunks = 4 * coarse // 2
    x, y = lax.axis_index("gx"), lax.axis_index("gy")
    device = x * gy + y
    per_owner = rows * gy
    has_left, has_right = y > 0, y < gy - 1
    gated = gx == 4 and span == 4 and gy % 2 == 0
    first_core = lax.rem(y, 2) == 0

    inputs = [
        pltpu.make_async_copy(source, target, local_sem.at[n])
        for n, (source, target) in enumerate((
            (new_row_hbm, new_row_ref), (a_cols_hbm, a_cols_ref), (p_cols_hbm, p_cols_ref),
            (a_hbm, a_ref), (p_hbm, p_ref)))]
    for copy in inputs:
        copy.start()

    barrier = pltpu.get_barrier_semaphore()
    for step in range(1, span):
        pl.semaphore_signal(
            barrier, inc=1, device_id={"gx": lax.rem(x + gx - step, gx)},
            device_id_type=pl.DeviceIdType.MESH)

    @pl.when(has_left)
    def _():
        pl.semaphore_signal(
            barrier, inc=1, device_id={"gy": y - 1}, device_id_type=pl.DeviceIdType.MESH)

    @pl.when(has_right)
    def _():
        pl.semaphore_signal(
            barrier, inc=1, device_id={"gy": y + 1}, device_id_type=pl.DeviceIdType.MESH)

    for copy in inputs[:3]:
        copy.wait()
    row_id = lax.broadcasted_iota(jnp.int32, (rows, LANES), 0)
    lane_id = lax.broadcasted_iota(jnp.int32, (rows, LANES), 1)
    filled = jnp.zeros((rows, LANES), jnp.int32)
    for row in range(rows):
        entries = [a_cols_ref[k, row] for k in range(A_TILES)]
        entries += [new_row_ref[row]]
        entries += [p_cols_ref[q, row] for q in range(P_TILES)]
        for lane, entry in enumerate(entries):
            filled = jnp.where((row_id == row) & (lane_id == lane), entry, filled)
    table[...] = filled
    table_from[0] = filled
    table_ext[1] = filled

    def put_rows(step, target, slot):
        owner = lax.rem(x + step, gx)
        for rank in range(CAP):
            row, _ = find_row(lambda r: new_row_ref[r], rows, per_owner, owner, rank)
            target[slot, rank] = a_ref[row]

    def a_copy(step):
        return pltpu.make_async_remote_copy(
            stage.at[step], recv.at[step], a_send.at[step], a_recv.at[step],
            device_id={"gx": lax.rem(x + step, gx)}, device_id_type=pl.DeviceIdType.MESH)

    def table_copy(step):
        return pltpu.make_async_remote_copy(
            table, table_from.at[step], t_send.at[step], t_recv.at[step],
            device_id={"gx": lax.rem(x + step, gx)}, device_id_type=pl.DeviceIdType.MESH)

    def halo_copies(side):
        target = y + 1 if side == 0 else y - 1
        place = 0 if side == 0 else 2
        return (
            pltpu.make_async_remote_copy(
                table, table_ext.at[place], ht_send.at[side], ht_recv.at[side],
                device_id={"gy": target}, device_id_type=pl.DeviceIdType.MESH),
            pltpu.make_async_remote_copy(
                p_hbm, ext.at[side], h_send.at[side], h_recv.at[side],
                device_id={"gy": target}, device_id_type=pl.DeviceIdType.MESH),
        )

    if gx == 4 and span == 4:
        odd = lax.rem(x, 2)
        send_order = [2, 3 - 2 * odd, 1 + 2 * odd]

        def arrival(n):
            later = n // 2
            return 2 * n * (1 - later) + later * (
                (1 - odd) * (3 - 2 * (n - 2)) + odd * (1 + 2 * (n - 2)))
    else:
        send_order = list(range(1, span))

        def arrival(n):
            return n

    for copy in inputs[3:]:
        copy.wait()
    put_rows(send_order[0], stage, send_order[0])
    greeted = span - 1 + jnp.where(has_left, 1, 0) + jnp.where(has_right, 1, 0)
    pl.semaphore_wait(barrier, greeted)
    a_copy(send_order[0]).start()
    for step in range(1, span):
        table_copy(step).start()

    @pl.when(has_right)
    def _():
        for copy in halo_copies(0):
            copy.start()

    @pl.when(has_left)
    def _():
        for copy in halo_copies(1):
            copy.start()

    for n, step in enumerate(send_order[1:]):
        put_rows(step, stage, step)
        if gated and n == 0:
            @pl.when(jnp.logical_not(first_core))
            def _():
                a_copy(step).start()
        else:
            a_copy(step).start()
    put_rows(0, recv, 0)

    def split_p(source, base):
        def body(row, carry):
            for q in range(P_TILES):
                high, low = split(source[row, q])
                columns = pl.ds(q * tile, tile)
                ext_cat[base + row, pl.ds(0, tile), columns] = high
                ext_cat[base + row, pl.ds(tile, tile), columns] = high
                ext_cat[base + row, pl.ds(2 * tile, tile), columns] = low
            return carry
        lax.fori_loop(0, rows, body, 0)

    def flip(row, carry):
        for q in range(P_TILES):
            flipped[row, q] = p_ref[row, q].T
        return carry

    lax.fori_loop(0, rows, flip, 0)
    split_p(p_ref, rows)

    def clear(n, carry):
        for t in range(coarse):
            own_ref[t, n] = jnp.zeros((tile, tile), jnp.float32)
            following[t, n] = jnp.zeros((tile, tile), jnp.float32)
        return carry

    lax.fori_loop(0, 4 * coarse, clear, 0)

    @pl.when(jnp.logical_not(has_left))
    def _():
        copy = pltpu.make_async_copy(following, arrived_ref, local_sem.at[0])
        copy.start()
        copy.wait()

    for step in range(1, span):
        table_copy(step).wait_recv()

    @pl.when(has_left)
    def _():
        for copy in halo_copies(0):
            copy.wait_recv()
        split_p(ext.at[0], 0)

    @pl.when(jnp.logical_not(has_left))
    def _():
        table_ext[0] = jnp.zeros((rows, LANES), jnp.int32)

    @pl.when(has_right)
    def _():
        for copy in halo_copies(1):
            copy.wait_recv()
        split_p(ext.at[1], 2 * rows)

    @pl.when(jnp.logical_not(has_right))
    def _():
        table_ext[2] = jnp.zeros((rows, LANES), jnp.int32)

    to_scalar = (
        pltpu.make_async_copy(table_from, from_s, local_sem.at[0]),
        pltpu.make_async_copy(table_ext, ext_s, local_sem.at[1]),
    )
    for copy in to_scalar:
        copy.start()
    for copy in to_scalar:
        copy.wait()

    def next_copy(n):
        piece = pl.ds(2 * n, 2)
        return pltpu.make_async_remote_copy(
            following.at[:, piece], arrived_ref.at[:, piece], n_send.at[n], n_recv.at[n],
            device_id={"gy": y + 1}, device_id_type=pl.DeviceIdType.MESH)

    def own_copy(n):
        piece = pl.ds(2 * n, 2)
        return pltpu.make_async_copy(own_ref.at[:, piece], own_out.at[:, piece], o_sem.at[n])

    def one_distance(n, carry):
        step = arrival(n)
        if gated:
            @pl.when((n == 1) & first_core)
            def _():
                pl.semaphore_wait(gate, 1)
                a_copy(send_order[1]).start()

            @pl.when((n == 1) & jnp.logical_not(first_core))
            def _():
                for sent in send_order[:2]:
                    a_copy(sent).wait_send()
                pl.semaphore_signal(
                    gate, inc=1, device_id={"gy": y - 1}, device_id_type=pl.DeviceIdType.MESH)

        @pl.when(n > 0)
        def _():
            a_copy(step).wait_recv()

        slots = []
        lifts = [[] for _ in range(2 * coarse)]
        for rank in range(CAP):
            row, there = find_row(
                lambda r: from_s[step, r, ROW_LANE], rows, per_owner, x, rank)
            own_row = lax.rem(from_s[step, row, ROW_LANE], jnp.int32(rows))
            wide = []
            for k in range(A_TILES):
                column = jnp.where(there, from_s[step, row, k] - (device - 1) * rows, rows)
                column = jnp.minimum(jnp.maximum(column, 0), 3 * rows - 1)
                for q in range(P_TILES):
                    goal = ext_s[lax.div(column, rows), lax.rem(column, rows), P_LANE + q]
                    wide.append(jnp.where(there, goal - (device - 1) * coarse, -1))
                high, low = split(recv[step, rank, k])
                left = jnp.concatenate([high, low, high], axis=1)
                products[rank, k] = jnp.dot(
                    left, ext_cat[column], preferred_element_type=jnp.float32)
            slots.append(wide)
            goals = [
                ext_s[1, own_row, P_LANE + p] - device * coarse for p in range(P_TILES)]
            for t in range(2 * coarse):
                lifts[t].append(sum(
                    jnp.where(goals[p] == t, 1.0, 0.0) * flipped[own_row, p]
                    for p in range(P_TILES)))
        lift_cat = []
        for t in range(2 * coarse):
            high, low = split(jnp.concatenate(lifts[t], axis=1))
            lift_cat.append(jnp.concatenate([high, low, high], axis=1))
        lift_cat = jnp.concatenate(lift_cat, axis=0)

        def one_chunk(c, carry):
            halves = []
            for q in range(2):
                w = 2 * c + q
                parts = []
                for rank in range(CAP):
                    total = None
                    for m in range(A_TILES * P_TILES):
                        k, p = m // P_TILES, m % P_TILES
                        weight = jnp.where(slots[rank][m] == w, 1.0, 0.0)
                        term = weight * products[rank, k, :, pl.ds(p * tile, tile)]
                        total = term if total is None else total + term
                    parts.append(total)
                high, low = split(jnp.concatenate(parts, axis=0))
                halves.append(jnp.concatenate([high, high, low], axis=0))
            right = jnp.concatenate(halves, axis=1)
            result = jnp.dot(lift_cat, right, preferred_element_type=jnp.float32)
            for t in range(2 * coarse):
                for q in range(2):
                    value = result[t * tile:(t + 1) * tile, q * tile:(q + 1) * tile]
                    if t < coarse:
                        own_ref[t, 2 * c + q] += value
                    else:
                        following[t - coarse, 2 * c + q] += value

            @pl.when((n == span - 1) & has_right)
            def _():
                next_copy(c).start()

            @pl.when(n == span - 1)
            def _():
                own_copy(c).start()

            return carry

        lax.fori_loop(0, chunks, one_chunk, 0)
        return carry

    lax.fori_loop(0, span, one_distance, 0)

    for step in range(1, span):
        table_copy(step).wait_send()
    if gated:
        @pl.when(first_core)
        def _():
            for step in send_order[:2]:
                a_copy(step).wait_send()

        a_copy(send_order[2]).wait_send()
    else:
        for step in send_order:
            a_copy(step).wait_send()

    for c in range(chunks):
        own_copy(c).wait()

    @pl.when(has_right)
    def _():
        for copy in halo_copies(0):
            copy.wait_send()
        for c in range(chunks):
            next_copy(c).wait_send()

    @pl.when(has_left)
    def _():
        for copy in halo_copies(1):
            copy.wait_send()
        for c in range(chunks):
            next_copy(c).wait_recv()


def shards(a_tiles, a_cols, new_row, p_tiles, p_cols):
    rows, tile = a_tiles.shape[0], a_tiles.shape[2]
    gx, gy = lax.axis_size("gx"), lax.axis_size("gy")
    span = min(SPAN, gx)
    coarse = rows // 4
    band = jax.ShapeDtypeStruct((coarse, 4 * coarse, tile, tile), jnp.float32)
    dma = pltpu.SemaphoreType.DMA
    row_block = (span, CAP, A_TILES, tile, tile)
    own, arrived = pl.pallas_call(
        functools.partial(kernel, span, gx, gy),
        out_shape=[band, band],
        in_specs=[pl.BlockSpec(memory_space=pl.ANY)] * 5,
        out_specs=[pl.BlockSpec(memory_space=pl.ANY)] * 2,
        scratch_shapes=[
            pltpu.VMEM(band.shape, jnp.float32),
            pltpu.SMEM((rows,), jnp.int32),
            pltpu.SMEM((A_TILES, rows), jnp.int32),
            pltpu.SMEM((P_TILES, rows), jnp.int32),
            pltpu.VMEM(a_tiles.shape, jnp.float32),
            pltpu.VMEM(p_tiles.shape, jnp.float32),
            pltpu.VMEM(row_block, jnp.float32),
            pltpu.VMEM(row_block, jnp.float32),
            pltpu.VMEM((2, rows, P_TILES, tile, tile), jnp.float32),
            pltpu.VMEM((3 * rows, 3 * tile, P_TILES * tile), jnp.bfloat16),
            pltpu.VMEM((rows, P_TILES, tile, tile), jnp.float32),
            pltpu.VMEM((CAP, A_TILES, tile, P_TILES * tile), jnp.float32),
            pltpu.VMEM((coarse, 4 * coarse, tile, tile), jnp.float32),
            pltpu.VMEM((rows, LANES), jnp.int32),
            pltpu.VMEM((span, rows, LANES), jnp.int32),
            pltpu.VMEM((3, rows, LANES), jnp.int32),
            pltpu.SMEM((span, rows, LANES), jnp.int32),
            pltpu.SMEM((3, rows, LANES), jnp.int32),
            dma((span,)), dma((span,)), dma((span,)), dma((span,)),
            dma((2,)), dma((2,)), dma((2,)), dma((2,)),
            dma((2 * coarse,)), dma((2 * coarse,)), dma((5,)),
            pltpu.SemaphoreType.REGULAR, dma((2 * coarse,)),
        ],
        compiler_params=pltpu.CompilerParams(
            collective_id=0, has_side_effects=True, vmem_limit_bytes=64 * 1024 * 1024),
        name="galerkin",
    )(new_row, a_cols.T, p_cols.T, a_tiles, p_tiles)
    pad = ((0, 0), (coarse, 0), (0, 0), (0, 0))
    behind = ((0, 0), (0, coarse), (0, 0), (0, 0))
    return jnp.pad(own, pad) + jnp.pad(arrived, behind)


def solution(mesh):
    in_specs = (
        P(("gx", "gy"), None, None, None),
        P(("gx", "gy"), None),
        P(("gx", "gy")),
        P(("gx", "gy"), None, None, None),
        P(("gx", "gy"), None),
    )
    out_specs = P(("gx", "gy"), None, None, None)
    return jax.shard_map(shards, mesh=mesh, in_specs=in_specs, out_specs=out_specs, check_vma=False)
```

```python
import functools

import jax
import jax.numpy as jnp
from jax import lax
from jax.experimental import pallas as pl
from jax.experimental.pallas import tpu as pltpu
from jax.sharding import PartitionSpec as P

A_TILES = 4
P_TILES = 2
CAP = 2
SPAN = 6
LANES = 128
ROW_LANE = A_TILES
P_LANE = A_TILES + 1


def split(value):
    high = value.astype(jnp.bfloat16)
    low = (value - high.astype(jnp.float32)).astype(jnp.bfloat16)
    return high, low


def find_row(new_row_of, rows, per_owner, owner, rank):
    seen = jnp.int32(0)
    found = jnp.int32(0)
    for row in range(rows):
        here = lax.div(new_row_of(row), jnp.int32(per_owner)) == owner
        found = jnp.where(here & (seen == rank), row, found)
        seen = seen + here.astype(jnp.int32)
    return found, seen > rank


def kernel(
    span, gx, gy,
    new_row_hbm, a_cols_hbm, p_cols_hbm, a_hbm, p_hbm,
    own_ref, arrived_ref,
    new_row_ref, a_cols_ref, p_cols_ref, a_ref, p_ref,
    stage, recv, ext, ext_cat, flipped, products, summed, lifted, following,
    table, table_from, table_ext, from_s, ext_s,
    a_send, a_recv, t_send, t_recv, h_send, h_recv, ht_send, ht_recv, n_send, n_recv, local_sem, gate,
):
    rows, tile = p_ref.shape[0], p_ref.shape[2]
    coarse = rows // 4
    chunks = 4 * coarse // 2
    x, y = lax.axis_index("gx"), lax.axis_index("gy")
    device = x * gy + y
    per_owner = rows * gy
    has_left, has_right = y > 0, y < gy - 1
    gated = gx == 4 and span == 4 and gy % 2 == 0
    first_core = lax.rem(y, 2) == 0

    inputs = [
        pltpu.make_async_copy(source, target, local_sem.at[n])
        for n, (source, target) in enumerate((
            (new_row_hbm, new_row_ref), (a_cols_hbm, a_cols_ref), (p_cols_hbm, p_cols_ref),
            (a_hbm, a_ref), (p_hbm, p_ref)))]
    for copy in inputs:
        copy.start()

    barrier = pltpu.get_barrier_semaphore()
    for step in range(1, span):
        pl.semaphore_signal(
            barrier, inc=1, device_id={"gx": lax.rem(x + gx - step, gx)},
            device_id_type=pl.DeviceIdType.MESH)

    @pl.when(has_left)
    def _():
        pl.semaphore_signal(
            barrier, inc=1, device_id={"gy": y - 1}, device_id_type=pl.DeviceIdType.MESH)

    @pl.when(has_right)
    def _():
        pl.semaphore_signal(
            barrier, inc=1, device_id={"gy": y + 1}, device_id_type=pl.DeviceIdType.MESH)

    for copy in inputs[:3]:
        copy.wait()
    row_id = lax.broadcasted_iota(jnp.int32, (rows, LANES), 0)
    lane_id = lax.broadcasted_iota(jnp.int32, (rows, LANES), 1)
    filled = jnp.zeros((rows, LANES), jnp.int32)
    for row in range(rows):
        entries = [a_cols_ref[k, row] for k in range(A_TILES)]
        entries += [new_row_ref[row]]
        entries += [p_cols_ref[q, row] for q in range(P_TILES)]
        for lane, entry in enumerate(entries):
            filled = jnp.where((row_id == row) & (lane_id == lane), entry, filled)
    table[...] = filled
    table_from[0] = filled
    table_ext[1] = filled

    def put_row(step, rank, target):
        owner = lax.rem(x + step, gx)
        row, _ = find_row(lambda r: new_row_ref[r], rows, per_owner, owner, rank)
        target[step, rank] = a_ref[row]

    def a_copy(step, rank):
        return pltpu.make_async_remote_copy(
            stage.at[step, rank], recv.at[step, rank],
            a_send.at[step, rank], a_recv.at[step, rank],
            device_id={"gx": lax.rem(x + step, gx)}, device_id_type=pl.DeviceIdType.MESH)

    def table_copy(step):
        return pltpu.make_async_remote_copy(
            table, table_from.at[step], t_send.at[step], t_recv.at[step],
            device_id={"gx": lax.rem(x + step, gx)}, device_id_type=pl.DeviceIdType.MESH)

    def halo_copies(side):
        target = y + 1 if side == 0 else y - 1
        place = 0 if side == 0 else 2
        return (
            pltpu.make_async_remote_copy(
                table, table_ext.at[place], ht_send.at[side], ht_recv.at[side],
                device_id={"gy": target}, device_id_type=pl.DeviceIdType.MESH),
            pltpu.make_async_remote_copy(
                p_hbm, ext.at[side], h_send.at[side], h_recv.at[side],
                device_id={"gy": target}, device_id_type=pl.DeviceIdType.MESH),
        )

    if gx == 4 and span == 4:
        odd = lax.rem(x, 2)
        send_order = [2, 3 - 2 * odd, 1 + 2 * odd]

        def arrival(n):
            later = n // 2
            return 2 * n * (1 - later) + later * (
                (1 - odd) * (3 - 2 * (n - 2)) + odd * (1 + 2 * (n - 2)))
    else:
        send_order = list(range(1, span))

        def arrival(n):
            return n

    for copy in inputs[3:]:
        copy.wait()
    put_row(send_order[0], 0, stage)
    greeted = span - 1 + jnp.where(has_left, 1, 0) + jnp.where(has_right, 1, 0)
    pl.semaphore_wait(barrier, greeted)
    a_copy(send_order[0], 0).start()
    put_row(send_order[0], 1, stage)
    a_copy(send_order[0], 1).start()
    for step in range(1, span):
        table_copy(step).start()

    @pl.when(has_right)
    def _():
        for copy in halo_copies(0):
            copy.start()

    @pl.when(has_left)
    def _():
        for copy in halo_copies(1):
            copy.start()

    held = send_order[1] if gated else None
    for step in reversed(send_order[1:]):
        for rank in range(CAP):
            put_row(step, rank, stage)
            if step is not held:
                a_copy(step, rank).start()
    for rank in range(CAP):
        put_row(0, rank, recv)

    def split_p(source, base):
        def body(row, carry):
            for q in range(P_TILES):
                high, low = split(source[row, q])
                columns = pl.ds(q * tile, tile)
                ext_cat[base + row, pl.ds(0, tile), columns] = high
                ext_cat[base + row, pl.ds(tile, tile), columns] = high
                ext_cat[base + row, pl.ds(2 * tile, tile), columns] = low
            return carry
        lax.fori_loop(0, rows, body, 0)

    def flip(row, carry):
        for q in range(P_TILES):
            flipped[row, q] = p_ref[row, q].T
        return carry

    lax.fori_loop(0, rows, flip, 0)
    split_p(p_ref, rows)

    def clear(n, carry):
        for t in range(coarse):
            own_ref[t, n] = jnp.zeros((tile, tile), jnp.float32)
            following[t, n] = jnp.zeros((tile, tile), jnp.float32)
        return carry

    lax.fori_loop(0, 4 * coarse, clear, 0)

    @pl.when(jnp.logical_not(has_left))
    def _():
        copy = pltpu.make_async_copy(following, arrived_ref, local_sem.at[0])
        copy.start()
        copy.wait()

    for step in range(1, span):
        table_copy(step).wait_recv()

    @pl.when(has_left)
    def _():
        for copy in halo_copies(0):
            copy.wait_recv()
        split_p(ext.at[0], 0)

    @pl.when(jnp.logical_not(has_left))
    def _():
        table_ext[0] = jnp.zeros((rows, LANES), jnp.int32)

    @pl.when(has_right)
    def _():
        for copy in halo_copies(1):
            copy.wait_recv()
        split_p(ext.at[1], 2 * rows)

    @pl.when(jnp.logical_not(has_right))
    def _():
        table_ext[2] = jnp.zeros((rows, LANES), jnp.int32)

    to_scalar = (
        pltpu.make_async_copy(table_from, from_s, local_sem.at[0]),
        pltpu.make_async_copy(table_ext, ext_s, local_sem.at[1]),
    )
    for copy in to_scalar:
        copy.start()
    for copy in to_scalar:
        copy.wait()

    def next_copy(n):
        piece = pl.ds(2 * n, 2)
        return pltpu.make_async_remote_copy(
            following.at[:, piece], arrived_ref.at[:, piece], n_send.at[n], n_recv.at[n],
            device_id={"gy": y + 1}, device_id_type=pl.DeviceIdType.MESH)

    def flow(n):
        def hand_on(rank):
            pl.semaphore_signal(
                gate.at[rank], inc=1, device_id={"gy": y - 1},
                device_id_type=pl.DeviceIdType.MESH)

        @pl.when((n == 1) & jnp.logical_not(first_core))
        def _():
            for rank in range(CAP):
                a_copy(send_order[0], rank).wait_send()
                a_copy(held, rank).start()

        @pl.when((n == span - 1) & jnp.logical_not(first_core))
        def _():
            for rank in range(CAP):
                a_copy(held, rank).wait_send()
                hand_on(rank)

        @pl.when((n == span - 1) & first_core)
        def _():
            for rank in range(CAP):
                pl.semaphore_wait(gate.at[rank], 1)
                a_copy(held, rank).start()

    def one_distance(n, carry):
        step = arrival(n)
        if gated:
            flow(n)

        lifts = [[] for _ in range(2 * coarse)]
        for rank in range(CAP):
            row, there = find_row(
                lambda r: from_s[step, r, ROW_LANE], rows, per_owner, x, rank)
            own_row = lax.rem(from_s[step, row, ROW_LANE], jnp.int32(rows))
            goals = [
                ext_s[1, own_row, P_LANE + p] - device * coarse for p in range(P_TILES)]
            for t in range(2 * coarse):
                lifts[t].append(sum(
                    jnp.where(goals[p] == t, 1.0, 0.0) * flipped[own_row, p]
                    for p in range(P_TILES)))
            wide, columns = [], []
            for k in range(A_TILES):
                column = jnp.where(there, from_s[step, row, k] - (device - 1) * rows, rows)
                column = jnp.minimum(jnp.maximum(column, 0), 3 * rows - 1)
                columns.append(column)
                for q in range(P_TILES):
                    goal = ext_s[lax.div(column, rows), lax.rem(column, rows), P_LANE + q]
                    wide.append(jnp.where(there, goal - (device - 1) * coarse, -1))

            @pl.when(n > 0)
            def _():
                a_copy(step, rank).wait_recv()

            for k in range(A_TILES):
                high, low = split(recv[step, rank, k])
                left = jnp.concatenate([high, low, high], axis=1)
                products[k] = jnp.dot(
                    left, ext_cat[columns[k]], preferred_element_type=jnp.float32)

            def gather(c, carry):
                for q in range(2):
                    total = None
                    for m in range(A_TILES * P_TILES):
                        k, p = m // P_TILES, m % P_TILES
                        weight = jnp.where(wide[m] == 2 * c + q, 1.0, 0.0)
                        term = weight * products[k, :, pl.ds(p * tile, tile)]
                        total = term if total is None else total + term
                    high, low = split(total)
                    here = pl.ds(q * tile, tile)
                    for part, value in enumerate((high, high, low)):
                        summed[c, pl.ds((part * CAP + rank) * tile, tile), here] = value
                return carry

            lax.fori_loop(0, chunks, gather, 0)

        for t in range(2 * coarse):
            high, low = split(jnp.concatenate(lifts[t], axis=1))
            lifted[pl.ds(t * tile, tile)] = jnp.concatenate([high, low, high], axis=1)

        def one_chunk(c, first, target):
            result = jnp.dot(
                lifted[pl.ds(first * tile, coarse * tile)], summed[c],
                preferred_element_type=jnp.float32)
            for t in range(coarse):
                for q in range(2):
                    target[t, 2 * c + q] += (
                        result[t * tile:(t + 1) * tile, q * tile:(q + 1) * tile])

        def next_chunk(c, carry):
            one_chunk(c, coarse, following)

            @pl.when((n == span - 1) & has_right)
            def _():
                next_copy(c).start()

            return carry

        def own_chunk(c, carry):
            one_chunk(c, 0, own_ref)
            return carry

        lax.fori_loop(0, chunks, next_chunk, 0)
        lax.fori_loop(0, chunks, own_chunk, 0)
        return carry

    lax.fori_loop(0, span, one_distance, 0)

    for step in range(1, span):
        table_copy(step).wait_send()
    for step in send_order:
        for rank in range(CAP):
            if gated and step is not send_order[2]:
                @pl.when(first_core)
                def _():
                    a_copy(step, rank).wait_send()
            else:
                a_copy(step, rank).wait_send()

    @pl.when(has_right)
    def _():
        for copy in halo_copies(0):
            copy.wait_send()
        for c in range(chunks):
            next_copy(c).wait_send()

    @pl.when(has_left)
    def _():
        for copy in halo_copies(1):
            copy.wait_send()
        for c in range(chunks):
            next_copy(c).wait_recv()


def shards(a_tiles, a_cols, new_row, p_tiles, p_cols):
    rows, tile = a_tiles.shape[0], a_tiles.shape[2]
    gx, gy = lax.axis_size("gx"), lax.axis_size("gy")
    span = min(SPAN, gx)
    coarse = rows // 4
    band = jax.ShapeDtypeStruct((coarse, 4 * coarse, tile, tile), jnp.float32)
    band_in = pltpu.VMEM(band.shape, jnp.float32)
    dma = pltpu.SemaphoreType.DMA
    row_block = (span, CAP, A_TILES, tile, tile)
    operands = [
        pltpu.with_memory_space_constraint(value, pltpu.HBM)
        for value in (new_row, a_cols.T, p_cols.T, a_tiles, p_tiles)]
    own, arrived = pl.pallas_call(
        functools.partial(kernel, span, gx, gy),
        out_shape=[band_in, band_in],
        in_specs=[pl.BlockSpec(memory_space=pl.ANY)] * 5,
        out_specs=[pl.BlockSpec(memory_space=pltpu.VMEM)] * 2,
        scratch_shapes=[
            pltpu.SMEM((rows,), jnp.int32),
            pltpu.SMEM((A_TILES, rows), jnp.int32),
            pltpu.SMEM((P_TILES, rows), jnp.int32),
            pltpu.VMEM(a_tiles.shape, jnp.float32),
            pltpu.VMEM(p_tiles.shape, jnp.float32),
            pltpu.VMEM(row_block, jnp.float32),
            pltpu.VMEM(row_block, jnp.float32),
            pltpu.VMEM((2, rows, P_TILES, tile, tile), jnp.float32),
            pltpu.VMEM((3 * rows, 3 * tile, P_TILES * tile), jnp.bfloat16),
            pltpu.VMEM((rows, P_TILES, tile, tile), jnp.float32),
            pltpu.VMEM((A_TILES, tile, P_TILES * tile), jnp.float32),
            pltpu.VMEM((2 * coarse, 3 * CAP * tile, 2 * tile), jnp.bfloat16),
            pltpu.VMEM((2 * coarse * tile, 3 * CAP * tile), jnp.bfloat16),
            pltpu.VMEM((coarse, 4 * coarse, tile, tile), jnp.float32),
            pltpu.VMEM((rows, LANES), jnp.int32),
            pltpu.VMEM((span, rows, LANES), jnp.int32),
            pltpu.VMEM((3, rows, LANES), jnp.int32),
            pltpu.SMEM((span, rows, LANES), jnp.int32),
            pltpu.SMEM((3, rows, LANES), jnp.int32),
            dma((span, CAP)), dma((span, CAP)), dma((span,)), dma((span,)),
            dma((2,)), dma((2,)), dma((2,)), dma((2,)),
            dma((2 * coarse,)), dma((2 * coarse,)), dma((5,)),
            pltpu.SemaphoreType.REGULAR((CAP,)),
        ],
        compiler_params=pltpu.CompilerParams(
            collective_id=0, has_side_effects=True, vmem_limit_bytes=48 * 1024 * 1024),
        name="galerkin",
    )(*operands)
    pad = ((0, 0), (coarse, 0), (0, 0), (0, 0))
    behind = ((0, 0), (0, coarse), (0, 0), (0, 0))
    return jnp.pad(own, pad) + jnp.pad(arrived, behind)


def solution(mesh):
    in_specs = (
        P(("gx", "gy"), None, None, None),
        P(("gx", "gy"), None),
        P(("gx", "gy")),
        P(("gx", "gy"), None, None, None),
        P(("gx", "gy"), None),
    )
    out_specs = P(("gx", "gy"), None, None, None)
    return jax.shard_map(shards, mesh=mesh, in_specs=in_specs, out_specs=out_specs, check_vma=False)
```

```python
import functools

import jax
import jax.numpy as jnp
from jax import lax
from jax.experimental import pallas as pl
from jax.experimental.pallas import tpu as pltpu
from jax.sharding import PartitionSpec as P

A_TILES = 4
P_TILES = 2
CAP = 2
SPAN = 6
LANES = 128
ROW_LANE = A_TILES
P_LANE = A_TILES + 1


def split(value):
    high = value.astype(jnp.bfloat16)
    low = (value - high.astype(jnp.float32)).astype(jnp.bfloat16)
    return high, low


def find_row(new_row_of, rows, per_owner, owner, rank):
    seen = jnp.int32(0)
    found = jnp.int32(0)
    for row in range(rows):
        here = lax.div(new_row_of(row), jnp.int32(per_owner)) == owner
        found = jnp.where(here & (seen == rank), row, found)
        seen = seen + here.astype(jnp.int32)
    return found, seen > rank


def kernel(
    span, gx, gy,
    new_row_hbm, a_cols_hbm, p_cols_hbm, a_hbm, p_hbm,
    own_ref, arrived_ref,
    new_row_ref, a_cols_ref, p_cols_ref, a_ref, p_ref,
    stage, recv, ext, ext_cat, flipped, products, summed, lifted, following,
    table, table_from, table_ext, from_s, ext_s,
    a_send, a_recv, t_send, t_recv, h_send, h_recv, ht_send, ht_recv, n_send, n_recv, local_sem, gate,
):
    rows, tile = p_ref.shape[0], p_ref.shape[2]
    coarse = rows // 4
    chunks = 4 * coarse // 2
    x, y = lax.axis_index("gx"), lax.axis_index("gy")
    device = x * gy + y
    per_owner = rows * gy
    has_left, has_right = y > 0, y < gy - 1
    gated = gx == 4 and span == 4 and gy % 2 == 0
    first_core = lax.rem(y, 2) == 0

    inputs = [
        pltpu.make_async_copy(source, target, local_sem.at[n])
        for n, (source, target) in enumerate((
            (new_row_hbm, new_row_ref), (a_cols_hbm, a_cols_ref), (p_cols_hbm, p_cols_ref),
            (a_hbm, a_ref), (p_hbm, p_ref)))]
    for copy in inputs:
        copy.start()

    barrier = pltpu.get_barrier_semaphore()
    for step in range(1, span):
        pl.semaphore_signal(
            barrier, inc=1, device_id={"gx": lax.rem(x + gx - step, gx)},
            device_id_type=pl.DeviceIdType.MESH)

    @pl.when(has_left)
    def _():
        pl.semaphore_signal(
            barrier, inc=1, device_id={"gy": y - 1}, device_id_type=pl.DeviceIdType.MESH)

    @pl.when(has_right)
    def _():
        pl.semaphore_signal(
            barrier, inc=1, device_id={"gy": y + 1}, device_id_type=pl.DeviceIdType.MESH)

    for copy in inputs[:3]:
        copy.wait()
    row_id = lax.broadcasted_iota(jnp.int32, (rows, LANES), 0)
    lane_id = lax.broadcasted_iota(jnp.int32, (rows, LANES), 1)
    filled = jnp.zeros((rows, LANES), jnp.int32)
    for row in range(rows):
        entries = [a_cols_ref[k, row] for k in range(A_TILES)]
        entries += [new_row_ref[row]]
        entries += [p_cols_ref[q, row] for q in range(P_TILES)]
        for lane, entry in enumerate(entries):
            filled = jnp.where((row_id == row) & (lane_id == lane), entry, filled)
    table[...] = filled
    table_from[0] = filled
    table_ext[1] = filled

    def put_row(step, rank, target):
        owner = lax.rem(x + step, gx)
        row, _ = find_row(lambda r: new_row_ref[r], rows, per_owner, owner, rank)
        target[step, rank] = a_ref[row]

    def a_copy(step, rank):
        return pltpu.make_async_remote_copy(
            stage.at[step, rank], recv.at[step, rank],
            a_send.at[step, rank], a_recv.at[step, rank],
            device_id={"gx": lax.rem(x + step, gx)}, device_id_type=pl.DeviceIdType.MESH)

    def table_copy(step):
        return pltpu.make_async_remote_copy(
            table, table_from.at[step], t_send.at[step], t_recv.at[step],
            device_id={"gx": lax.rem(x + step, gx)}, device_id_type=pl.DeviceIdType.MESH)

    def halo_copies(side):
        target = y + 1 if side == 0 else y - 1
        place = 0 if side == 0 else 2
        return (
            pltpu.make_async_remote_copy(
                table, table_ext.at[place], ht_send.at[side], ht_recv.at[side],
                device_id={"gy": target}, device_id_type=pl.DeviceIdType.MESH),
            pltpu.make_async_remote_copy(
                p_hbm, ext.at[side], h_send.at[side], h_recv.at[side],
                device_id={"gy": target}, device_id_type=pl.DeviceIdType.MESH),
        )

    if gx == 4 and span == 4:
        odd = lax.rem(x, 2)
        send_order = [2, 3 - 2 * odd, 1 + 2 * odd]

        def arrival(n):
            later = n // 2
            return 2 * n * (1 - later) + later * (
                (1 - odd) * (3 - 2 * (n - 2)) + odd * (1 + 2 * (n - 2)))
    else:
        send_order = list(range(1, span))

        def arrival(n):
            return n

    for copy in inputs[3:]:
        copy.wait()
    put_row(send_order[0], 0, stage)
    greeted = span - 1 + jnp.where(has_left, 1, 0) + jnp.where(has_right, 1, 0)
    pl.semaphore_wait(barrier, greeted)
    a_copy(send_order[0], 0).start()
    put_row(send_order[0], 1, stage)
    a_copy(send_order[0], 1).start()
    for step in range(1, span):
        table_copy(step).start()

    @pl.when(has_right)
    def _():
        for copy in halo_copies(0):
            copy.start()

    @pl.when(has_left)
    def _():
        for copy in halo_copies(1):
            copy.start()

    held = send_order[1] if gated else None
    for step in send_order[1:]:
        for rank in range(CAP):
            put_row(step, rank, stage)
            if step is held:
                @pl.when(jnp.logical_not(first_core))
                def _():
                    a_copy(step, rank).start()
            else:
                a_copy(step, rank).start()
    for rank in range(CAP):
        put_row(0, rank, recv)

    def split_p(source, base):
        def body(row, carry):
            for q in range(P_TILES):
                high, low = split(source[row, q])
                columns = pl.ds(q * tile, tile)
                ext_cat[base + row, pl.ds(0, tile), columns] = high
                ext_cat[base + row, pl.ds(tile, tile), columns] = high
                ext_cat[base + row, pl.ds(2 * tile, tile), columns] = low
            return carry
        lax.fori_loop(0, rows, body, 0)

    def flip(row, carry):
        for q in range(P_TILES):
            flipped[row, q] = p_ref[row, q].T
        return carry

    lax.fori_loop(0, rows, flip, 0)
    split_p(p_ref, rows)

    def clear(n, carry):
        for t in range(coarse):
            own_ref[t, n] = jnp.zeros((tile, tile), jnp.float32)
            following[t, n] = jnp.zeros((tile, tile), jnp.float32)
        return carry

    lax.fori_loop(0, 4 * coarse, clear, 0)

    @pl.when(jnp.logical_not(has_left))
    def _():
        copy = pltpu.make_async_copy(following, arrived_ref, local_sem.at[0])
        copy.start()
        copy.wait()

    for step in range(1, span):
        table_copy(step).wait_recv()

    @pl.when(has_left)
    def _():
        for copy in halo_copies(0):
            copy.wait_recv()
        split_p(ext.at[0], 0)

    @pl.when(jnp.logical_not(has_left))
    def _():
        table_ext[0] = jnp.zeros((rows, LANES), jnp.int32)

    @pl.when(has_right)
    def _():
        for copy in halo_copies(1):
            copy.wait_recv()
        split_p(ext.at[1], 2 * rows)

    @pl.when(jnp.logical_not(has_right))
    def _():
        table_ext[2] = jnp.zeros((rows, LANES), jnp.int32)

    to_scalar = (
        pltpu.make_async_copy(table_from, from_s, local_sem.at[0]),
        pltpu.make_async_copy(table_ext, ext_s, local_sem.at[1]),
    )
    for copy in to_scalar:
        copy.start()
    for copy in to_scalar:
        copy.wait()

    def next_copy(n):
        piece = pl.ds(2 * n, 2)
        return pltpu.make_async_remote_copy(
            following.at[:, piece], arrived_ref.at[:, piece], n_send.at[n], n_recv.at[n],
            device_id={"gy": y + 1}, device_id_type=pl.DeviceIdType.MESH)

    def flow(n):
        def hand_on(rank):
            pl.semaphore_signal(
                gate.at[rank], inc=1, device_id={"gy": y - 1},
                device_id_type=pl.DeviceIdType.MESH)

        @pl.when((n == 1) & jnp.logical_not(first_core))
        def _():
            for rank in range(CAP):
                a_copy(send_order[0], rank).wait_send()
            for rank in range(CAP):
                a_copy(held, rank).wait_send()
                hand_on(rank)

        @pl.when((n == 1) & first_core)
        def _():
            for rank in range(CAP):
                pl.semaphore_wait(gate.at[rank], 1)
                a_copy(held, rank).start()

    def one_distance(n, carry):
        step = arrival(n)
        if gated:
            flow(n)

        lifts = [[] for _ in range(2 * coarse)]
        for rank in range(CAP):
            row, there = find_row(
                lambda r: from_s[step, r, ROW_LANE], rows, per_owner, x, rank)
            own_row = lax.rem(from_s[step, row, ROW_LANE], jnp.int32(rows))
            goals = [
                ext_s[1, own_row, P_LANE + p] - device * coarse for p in range(P_TILES)]
            for t in range(2 * coarse):
                lifts[t].append(sum(
                    jnp.where(goals[p] == t, 1.0, 0.0) * flipped[own_row, p]
                    for p in range(P_TILES)))
            wide, columns = [], []
            for k in range(A_TILES):
                column = jnp.where(there, from_s[step, row, k] - (device - 1) * rows, rows)
                column = jnp.minimum(jnp.maximum(column, 0), 3 * rows - 1)
                columns.append(column)
                for q in range(P_TILES):
                    goal = ext_s[lax.div(column, rows), lax.rem(column, rows), P_LANE + q]
                    wide.append(jnp.where(there, goal - (device - 1) * coarse, -1))

            @pl.when(n > 0)
            def _():
                a_copy(step, rank).wait_recv()

            for k in range(A_TILES):
                high, low = split(recv[step, rank, k])
                left = jnp.concatenate([high, low, high], axis=1)
                products[k] = jnp.dot(
                    left, ext_cat[columns[k]], preferred_element_type=jnp.float32)

            def gather(c, carry):
                for q in range(2):
                    total = None
                    for m in range(A_TILES * P_TILES):
                        k, p = m // P_TILES, m % P_TILES
                        weight = jnp.where(wide[m] == 2 * c + q, 1.0, 0.0)
                        term = weight * products[k, :, pl.ds(p * tile, tile)]
                        total = term if total is None else total + term
                    high, low = split(total)
                    here = pl.ds(q * tile, tile)
                    for part, value in enumerate((high, high, low)):
                        summed[c, pl.ds((part * CAP + rank) * tile, tile), here] = value
                return carry

            lax.fori_loop(0, chunks, gather, 0)

        for t in range(2 * coarse):
            high, low = split(jnp.concatenate(lifts[t], axis=1))
            lifted[pl.ds(t * tile, tile)] = jnp.concatenate([high, low, high], axis=1)

        def one_chunk(c, first, target):
            result = jnp.dot(
                lifted[pl.ds(first * tile, coarse * tile)], summed[c],
                preferred_element_type=jnp.float32)
            for t in range(coarse):
                for q in range(2):
                    target[t, 2 * c + q] += (
                        result[t * tile:(t + 1) * tile, q * tile:(q + 1) * tile])

        def next_chunk(c, carry):
            one_chunk(c, coarse, following)

            @pl.when((n == span - 1) & has_right)
            def _():
                next_copy(c).start()

            return carry

        def own_chunk(c, carry):
            one_chunk(c, 0, own_ref)
            return carry

        lax.fori_loop(0, chunks, next_chunk, 0)
        lax.fori_loop(0, chunks, own_chunk, 0)
        return carry

    lax.fori_loop(0, span, one_distance, 0)

    for step in range(1, span):
        table_copy(step).wait_send()
    for step in send_order:
        for rank in range(CAP):
            if gated and step is not send_order[2]:
                @pl.when(first_core)
                def _():
                    a_copy(step, rank).wait_send()
            else:
                a_copy(step, rank).wait_send()

    @pl.when(has_right)
    def _():
        for copy in halo_copies(0):
            copy.wait_send()
        for c in range(chunks):
            next_copy(c).wait_send()

    @pl.when(has_left)
    def _():
        for copy in halo_copies(1):
            copy.wait_send()
        for c in range(chunks):
            next_copy(c).wait_recv()


def shards(a_tiles, a_cols, new_row, p_tiles, p_cols):
    rows, tile = a_tiles.shape[0], a_tiles.shape[2]
    gx, gy = lax.axis_size("gx"), lax.axis_size("gy")
    span = min(SPAN, gx)
    coarse = rows // 4
    band = jax.ShapeDtypeStruct((coarse, 4 * coarse, tile, tile), jnp.float32)
    band_in = pltpu.VMEM(band.shape, jnp.float32)
    dma = pltpu.SemaphoreType.DMA
    row_block = (span, CAP, A_TILES, tile, tile)
    operands = [
        pltpu.with_memory_space_constraint(value, pltpu.HBM)
        for value in (new_row, a_cols.T, p_cols.T, a_tiles, p_tiles)]
    own, arrived = pl.pallas_call(
        functools.partial(kernel, span, gx, gy),
        out_shape=[band_in, band_in],
        in_specs=[pl.BlockSpec(memory_space=pl.ANY)] * 5,
        out_specs=[pl.BlockSpec(memory_space=pltpu.VMEM)] * 2,
        scratch_shapes=[
            pltpu.SMEM((rows,), jnp.int32),
            pltpu.SMEM((A_TILES, rows), jnp.int32),
            pltpu.SMEM((P_TILES, rows), jnp.int32),
            pltpu.VMEM(a_tiles.shape, jnp.float32),
            pltpu.VMEM(p_tiles.shape, jnp.float32),
            pltpu.VMEM(row_block, jnp.float32),
            pltpu.VMEM(row_block, jnp.float32),
            pltpu.VMEM((2, rows, P_TILES, tile, tile), jnp.float32),
            pltpu.VMEM((3 * rows, 3 * tile, P_TILES * tile), jnp.bfloat16),
            pltpu.VMEM((rows, P_TILES, tile, tile), jnp.float32),
            pltpu.VMEM((A_TILES, tile, P_TILES * tile), jnp.float32),
            pltpu.VMEM((2 * coarse, 3 * CAP * tile, 2 * tile), jnp.bfloat16),
            pltpu.VMEM((2 * coarse * tile, 3 * CAP * tile), jnp.bfloat16),
            pltpu.VMEM((coarse, 4 * coarse, tile, tile), jnp.float32),
            pltpu.VMEM((rows, LANES), jnp.int32),
            pltpu.VMEM((span, rows, LANES), jnp.int32),
            pltpu.VMEM((3, rows, LANES), jnp.int32),
            pltpu.SMEM((span, rows, LANES), jnp.int32),
            pltpu.SMEM((3, rows, LANES), jnp.int32),
            dma((span, CAP)), dma((span, CAP)), dma((span,)), dma((span,)),
            dma((2,)), dma((2,)), dma((2,)), dma((2,)),
            dma((2 * coarse,)), dma((2 * coarse,)), dma((5,)),
            pltpu.SemaphoreType.REGULAR((CAP,)),
        ],
        compiler_params=pltpu.CompilerParams(
            collective_id=0, has_side_effects=True, vmem_limit_bytes=48 * 1024 * 1024),
        name="galerkin",
    )(*operands)
    pad = ((0, 0), (coarse, 0), (0, 0), (0, 0))
    behind = ((0, 0), (0, coarse), (0, 0), (0, 0))
    return jnp.pad(own, pad) + jnp.pad(arrived, behind)


def solution(mesh):
    in_specs = (
        P(("gx", "gy"), None, None, None),
        P(("gx", "gy"), None),
        P(("gx", "gy")),
        P(("gx", "gy"), None, None, None),
        P(("gx", "gy"), None),
    )
    out_specs = P(("gx", "gy"), None, None, None)
    return jax.shard_map(shards, mesh=mesh, in_specs=in_specs, out_specs=out_specs, check_vma=False)
```

```python
import functools

import jax
import jax.numpy as jnp
from jax import lax
from jax.experimental import pallas as pl
from jax.experimental.pallas import tpu as pltpu
from jax.sharding import PartitionSpec as P

A_TILES = 4
P_TILES = 2
CAP = 2
SPAN = 6
LANES = 128
ROW_LANE = A_TILES
P_LANE = A_TILES + 1


def split(value):
    high = value.astype(jnp.bfloat16)
    low = (value - high.astype(jnp.float32)).astype(jnp.bfloat16)
    return high, low


def find_row(new_row_of, rows, per_owner, owner, rank):
    seen = jnp.int32(0)
    found = jnp.int32(0)
    for row in range(rows):
        here = lax.div(new_row_of(row), jnp.int32(per_owner)) == owner
        found = jnp.where(here & (seen == rank), row, found)
        seen = seen + here.astype(jnp.int32)
    return found, seen > rank


def kernel(
    span, gx, gy,
    new_row_hbm, a_cols_hbm, p_cols_hbm, a_hbm, p_hbm,
    own_ref, arrived_ref,
    new_row_ref, a_cols_ref, p_cols_ref, a_ref, p_ref,
    stage, recv, ext, ext_cat, flipped, products, following,
    table, table_from, table_ext, from_s, ext_s,
    a_send, a_recv, t_send, t_recv, h_send, h_recv, ht_send, ht_recv, n_send, n_recv, local_sem, gate,
):
    rows, tile = p_ref.shape[0], p_ref.shape[2]
    coarse = rows // 4
    chunks = 4 * coarse // 2
    x, y = lax.axis_index("gx"), lax.axis_index("gy")
    device = x * gy + y
    per_owner = rows * gy
    has_left, has_right = y > 0, y < gy - 1
    gated = gx == 4 and span == 4 and gy % 2 == 0
    first_core = lax.rem(y, 2) == 0

    inputs = [
        pltpu.make_async_copy(source, target, local_sem.at[n])
        for n, (source, target) in enumerate((
            (new_row_hbm, new_row_ref), (a_cols_hbm, a_cols_ref), (p_cols_hbm, p_cols_ref),
            (a_hbm, a_ref), (p_hbm, p_ref)))]
    for copy in inputs:
        copy.start()

    barrier = pltpu.get_barrier_semaphore()
    for step in range(1, span):
        pl.semaphore_signal(
            barrier, inc=1, device_id={"gx": lax.rem(x + gx - step, gx)},
            device_id_type=pl.DeviceIdType.MESH)

    @pl.when(has_left)
    def _():
        pl.semaphore_signal(
            barrier, inc=1, device_id={"gy": y - 1}, device_id_type=pl.DeviceIdType.MESH)

    @pl.when(has_right)
    def _():
        pl.semaphore_signal(
            barrier, inc=1, device_id={"gy": y + 1}, device_id_type=pl.DeviceIdType.MESH)

    for copy in inputs[:3]:
        copy.wait()
    row_id = lax.broadcasted_iota(jnp.int32, (rows, LANES), 0)
    lane_id = lax.broadcasted_iota(jnp.int32, (rows, LANES), 1)
    filled = jnp.zeros((rows, LANES), jnp.int32)
    for row in range(rows):
        entries = [a_cols_ref[k, row] for k in range(A_TILES)]
        entries += [new_row_ref[row]]
        entries += [p_cols_ref[q, row] for q in range(P_TILES)]
        for lane, entry in enumerate(entries):
            filled = jnp.where((row_id == row) & (lane_id == lane), entry, filled)
    table[...] = filled
    table_from[0] = filled
    table_ext[1] = filled

    def put_row(step, rank, target):
        owner = lax.rem(x + step, gx)
        row, _ = find_row(lambda r: new_row_ref[r], rows, per_owner, owner, rank)
        target[step, rank] = a_ref[row]

    def a_copy(step, rank):
        return pltpu.make_async_remote_copy(
            stage.at[step, rank], recv.at[step, rank],
            a_send.at[step, rank], a_recv.at[step, rank],
            device_id={"gx": lax.rem(x + step, gx)}, device_id_type=pl.DeviceIdType.MESH)

    def table_copy(step):
        return pltpu.make_async_remote_copy(
            table, table_from.at[step], t_send.at[step], t_recv.at[step],
            device_id={"gx": lax.rem(x + step, gx)}, device_id_type=pl.DeviceIdType.MESH)

    def halo_copies(side):
        target = y + 1 if side == 0 else y - 1
        place = 0 if side == 0 else 2
        return (
            pltpu.make_async_remote_copy(
                table, table_ext.at[place], ht_send.at[side], ht_recv.at[side],
                device_id={"gy": target}, device_id_type=pl.DeviceIdType.MESH),
            pltpu.make_async_remote_copy(
                p_hbm, ext.at[side], h_send.at[side], h_recv.at[side],
                device_id={"gy": target}, device_id_type=pl.DeviceIdType.MESH),
        )

    if gx == 4 and span == 4:
        odd = lax.rem(x, 2)
        send_order = [2, 3 - 2 * odd, 1 + 2 * odd]

        def arrival(n):
            return lax.rem(4 + (2 * odd - 1) * n, 4)
    else:
        send_order = list(range(1, span))

        def arrival(n):
            return n

    for copy in inputs[3:]:
        copy.wait()
    put_row(send_order[0], 0, stage)
    greeted = span - 1 + jnp.where(has_left, 1, 0) + jnp.where(has_right, 1, 0)
    pl.semaphore_wait(barrier, greeted)
    def send_row(step, rank):
        if gated and step is not send_order[2]:
            @pl.when(jnp.logical_not(first_core))
            def _():
                a_copy(step, rank).start()
        else:
            a_copy(step, rank).start()

    send_row(send_order[0], 0)
    put_row(send_order[0], 1, stage)
    send_row(send_order[0], 1)
    for step in range(1, span):
        table_copy(step).start()

    @pl.when(has_right)
    def _():
        for copy in halo_copies(0):
            copy.start()

    @pl.when(has_left)
    def _():
        for copy in halo_copies(1):
            copy.start()

    for step in send_order[1:]:
        for rank in range(CAP):
            put_row(step, rank, stage)
            send_row(step, rank)
    for rank in range(CAP):
        put_row(0, rank, recv)

    def split_p(source, base):
        def body(row, carry):
            for q in range(P_TILES):
                high, low = split(source[row, q])
                columns = pl.ds(q * tile, tile)
                ext_cat[base + row, pl.ds(0, tile), columns] = high
                ext_cat[base + row, pl.ds(tile, tile), columns] = high
                ext_cat[base + row, pl.ds(2 * tile, tile), columns] = low
            return carry
        lax.fori_loop(0, rows, body, 0)

    def flip(row, carry):
        for q in range(P_TILES):
            flipped[row, q] = p_ref[row, q].T
        return carry

    lax.fori_loop(0, rows, flip, 0)
    split_p(p_ref, rows)

    def clear(n, carry):
        for t in range(coarse):
            own_ref[t, n] = jnp.zeros((tile, tile), jnp.float32)
            following[t, n] = jnp.zeros((tile, tile), jnp.float32)
        return carry

    lax.fori_loop(0, 4 * coarse, clear, 0)

    @pl.when(jnp.logical_not(has_left))
    def _():
        copy = pltpu.make_async_copy(following, arrived_ref, local_sem.at[0])
        copy.start()
        copy.wait()

    for step in range(1, span):
        table_copy(step).wait_recv()

    @pl.when(has_left)
    def _():
        for copy in halo_copies(0):
            copy.wait_recv()
        split_p(ext.at[0], 0)

    @pl.when(jnp.logical_not(has_left))
    def _():
        table_ext[0] = jnp.zeros((rows, LANES), jnp.int32)

    @pl.when(has_right)
    def _():
        for copy in halo_copies(1):
            copy.wait_recv()
        split_p(ext.at[1], 2 * rows)

    @pl.when(jnp.logical_not(has_right))
    def _():
        table_ext[2] = jnp.zeros((rows, LANES), jnp.int32)

    to_scalar = (
        pltpu.make_async_copy(table_from, from_s, local_sem.at[0]),
        pltpu.make_async_copy(table_ext, ext_s, local_sem.at[1]),
    )
    for copy in to_scalar:
        copy.start()
    for copy in to_scalar:
        copy.wait()

    def next_copy(n):
        piece = pl.ds(2 * n, 2)
        return pltpu.make_async_remote_copy(
            following.at[:, piece], arrived_ref.at[:, piece], n_send.at[n], n_recv.at[n],
            device_id={"gy": y + 1}, device_id_type=pl.DeviceIdType.MESH)

    def flow(n):
        @pl.when((n == 1) & jnp.logical_not(first_core))
        def _():
            for pair, step in enumerate(send_order[:2]):
                for rank in range(CAP):
                    a_copy(step, rank).wait_send()
                pl.semaphore_signal(
                    gate.at[pair], inc=1, device_id={"gy": y - 1},
                    device_id_type=pl.DeviceIdType.MESH)

        @pl.when((n == 1) & first_core)
        def _():
            for pair, step in enumerate(send_order[:2]):
                pl.semaphore_wait(gate.at[pair], 1)
                for rank in range(CAP):
                    a_copy(step, rank).start()

    def one_distance(n, carry):
        step = arrival(n)
        if gated:
            flow(n)

        slots = []
        lifts = [[] for _ in range(2 * coarse)]
        for rank in range(CAP):
            row, there = find_row(
                lambda r: from_s[step, r, ROW_LANE], rows, per_owner, x, rank)
            own_row = lax.rem(from_s[step, row, ROW_LANE], jnp.int32(rows))
            goals = [
                ext_s[1, own_row, P_LANE + p] - device * coarse for p in range(P_TILES)]
            for t in range(2 * coarse):
                lifts[t].append(sum(
                    jnp.where(goals[p] == t, 1.0, 0.0) * flipped[own_row, p]
                    for p in range(P_TILES)))
            wide, columns = [], []
            for k in range(A_TILES):
                column = jnp.where(there, from_s[step, row, k] - (device - 1) * rows, rows)
                column = jnp.minimum(jnp.maximum(column, 0), 3 * rows - 1)
                columns.append(column)
                for q in range(P_TILES):
                    goal = ext_s[lax.div(column, rows), lax.rem(column, rows), P_LANE + q]
                    wide.append(jnp.where(there, goal - (device - 1) * coarse, -1))

            @pl.when(n > 0)
            def _():
                a_copy(step, rank).wait_recv()

            slots.append(wide)
            for k in range(A_TILES):
                high, low = split(recv[step, rank, k])
                left = jnp.concatenate([high, low, high], axis=1)
                products[rank, k] = jnp.dot(
                    left, ext_cat[columns[k]], preferred_element_type=jnp.float32)

        lift_cat = []
        for t in range(2 * coarse):
            high, low = split(jnp.concatenate(lifts[t], axis=1))
            lift_cat.append(jnp.concatenate([high, low, high], axis=1))
        lift_cat = jnp.concatenate(lift_cat, axis=0)

        def one_chunk(c, carry):
            halves = []
            for q in range(2):
                w = 2 * c + q
                parts = []
                for rank in range(CAP):
                    total = None
                    for m in range(A_TILES * P_TILES):
                        k, p = m // P_TILES, m % P_TILES
                        weight = jnp.where(slots[rank][m] == w, 1.0, 0.0)
                        term = weight * products[rank, k, :, pl.ds(p * tile, tile)]
                        total = term if total is None else total + term
                    parts.append(total)
                high, low = split(jnp.concatenate(parts, axis=0))
                halves.append(jnp.concatenate([high, high, low], axis=0))
            right = jnp.concatenate(halves, axis=1)
            result = jnp.dot(lift_cat, right, preferred_element_type=jnp.float32)
            for t in range(2 * coarse):
                for q in range(2):
                    value = result[t * tile:(t + 1) * tile, q * tile:(q + 1) * tile]
                    if t < coarse:
                        own_ref[t, 2 * c + q] += value
                    else:
                        following[t - coarse, 2 * c + q] += value

            @pl.when((n == span - 1) & has_right)
            def _():
                next_copy(c).start()

            return carry

        lax.fori_loop(0, chunks, one_chunk, 0)
        return carry

    lax.fori_loop(0, span, one_distance, 0)

    for step in range(1, span):
        table_copy(step).wait_send()
    for step in send_order:
        for rank in range(CAP):
            if gated and step is not send_order[2]:
                @pl.when(first_core)
                def _():
                    a_copy(step, rank).wait_send()
            else:
                a_copy(step, rank).wait_send()

    @pl.when(has_right)
    def _():
        for copy in halo_copies(0):
            copy.wait_send()
        for c in range(chunks):
            next_copy(c).wait_send()

    @pl.when(has_left)
    def _():
        for copy in halo_copies(1):
            copy.wait_send()
        for c in range(chunks):
            next_copy(c).wait_recv()


def shards(a_tiles, a_cols, new_row, p_tiles, p_cols):
    rows, tile = a_tiles.shape[0], a_tiles.shape[2]
    gx, gy = lax.axis_size("gx"), lax.axis_size("gy")
    span = min(SPAN, gx)
    coarse = rows // 4
    band = jax.ShapeDtypeStruct((coarse, 4 * coarse, tile, tile), jnp.float32)
    band_in = pltpu.VMEM(band.shape, jnp.float32)
    dma = pltpu.SemaphoreType.DMA
    row_block = (span, CAP, A_TILES, tile, tile)
    operands = [
        pltpu.with_memory_space_constraint(value, pltpu.HBM)
        for value in (new_row, a_cols.T, p_cols.T, a_tiles, p_tiles)]
    own, arrived = pl.pallas_call(
        functools.partial(kernel, span, gx, gy),
        out_shape=[band_in, band_in],
        in_specs=[pl.BlockSpec(memory_space=pl.ANY)] * 5,
        out_specs=[pl.BlockSpec(memory_space=pltpu.VMEM)] * 2,
        scratch_shapes=[
            pltpu.SMEM((rows,), jnp.int32),
            pltpu.SMEM((A_TILES, rows), jnp.int32),
            pltpu.SMEM((P_TILES, rows), jnp.int32),
            pltpu.VMEM(a_tiles.shape, jnp.float32),
            pltpu.VMEM(p_tiles.shape, jnp.float32),
            pltpu.VMEM(row_block, jnp.float32),
            pltpu.VMEM(row_block, jnp.float32),
            pltpu.VMEM((2, rows, P_TILES, tile, tile), jnp.float32),
            pltpu.VMEM((3 * rows, 3 * tile, P_TILES * tile), jnp.bfloat16),
            pltpu.VMEM((rows, P_TILES, tile, tile), jnp.float32),
            pltpu.VMEM((CAP, A_TILES, tile, P_TILES * tile), jnp.float32),
            pltpu.VMEM((coarse, 4 * coarse, tile, tile), jnp.float32),
            pltpu.VMEM((rows, LANES), jnp.int32),
            pltpu.VMEM((span, rows, LANES), jnp.int32),
            pltpu.VMEM((3, rows, LANES), jnp.int32),
            pltpu.SMEM((span, rows, LANES), jnp.int32),
            pltpu.SMEM((3, rows, LANES), jnp.int32),
            dma((span, CAP)), dma((span, CAP)), dma((span,)), dma((span,)),
            dma((2,)), dma((2,)), dma((2,)), dma((2,)),
            dma((2 * coarse,)), dma((2 * coarse,)), dma((5,)),
            pltpu.SemaphoreType.REGULAR((2,)),
        ],
        compiler_params=pltpu.CompilerParams(
            collective_id=0, has_side_effects=True, vmem_limit_bytes=48 * 1024 * 1024),
        name="galerkin",
    )(*operands)
    pad = ((0, 0), (coarse, 0), (0, 0), (0, 0))
    behind = ((0, 0), (0, coarse), (0, 0), (0, 0))
    return jnp.pad(own, pad) + jnp.pad(arrived, behind)


def solution(mesh):
    in_specs = (
        P(("gx", "gy"), None, None, None),
        P(("gx", "gy"), None),
        P(("gx", "gy")),
        P(("gx", "gy"), None, None, None),
        P(("gx", "gy"), None),
    )
    out_specs = P(("gx", "gy"), None, None, None)
    return jax.shard_map(shards, mesh=mesh, in_specs=in_specs, out_specs=out_specs, check_vma=False)
```

```python
import functools

import jax
import jax.numpy as jnp
from jax import lax
from jax.experimental import pallas as pl
from jax.experimental.pallas import tpu as pltpu
from jax.sharding import PartitionSpec as P

A_TILES = 4
P_TILES = 2
CAP = 2
SPAN = 6
LANES = 128
ROW_LANE = A_TILES
P_LANE = A_TILES + 1


def split(value):
    high = value.astype(jnp.bfloat16)
    low = (value - high.astype(jnp.float32)).astype(jnp.bfloat16)
    return high, low


def find_row(new_row_of, rows, per_owner, owner, rank):
    seen = jnp.int32(0)
    found = jnp.int32(0)
    for row in range(rows):
        here = lax.div(new_row_of(row), jnp.int32(per_owner)) == owner
        found = jnp.where(here & (seen == rank), row, found)
        seen = seen + here.astype(jnp.int32)
    return found, seen > rank


def may_reach(k, p, place):
    columns = (1,) if k == 0 else (0, 1, 2)
    if p == 0:
        return place in columns
    return place - 1 in columns or place == 1


def kernel(
    span, gx, gy,
    new_row_hbm, a_cols_hbm, p_cols_hbm, a_hbm, p_hbm,
    own_ref, arrived_ref,
    new_row_ref, a_cols_ref, p_cols_ref, a_ref, p_ref,
    stage, recv, ext, ext_cat, flipped, products, following,
    table, table_from, table_ext, from_s, ext_s,
    a_send, a_recv, t_send, t_recv, h_send, h_recv, ht_send, ht_recv, n_send, n_recv, local_sem,
):
    rows, tile = p_ref.shape[0], p_ref.shape[2]
    coarse = rows // 4
    chunks = 4 * coarse // 2
    x, y = lax.axis_index("gx"), lax.axis_index("gy")
    device = x * gy + y
    per_owner = rows * gy
    has_left, has_right = y > 0, y < gy - 1
    paced = gx == 4 and span == 4 and gy % 2 == 0
    first_core = lax.rem(y, 2) == 0

    inputs = [
        pltpu.make_async_copy(source, target, local_sem.at[n])
        for n, (source, target) in enumerate((
            (new_row_hbm, new_row_ref), (a_cols_hbm, a_cols_ref), (p_cols_hbm, p_cols_ref),
            (a_hbm, a_ref), (p_hbm, p_ref)))]
    for copy in inputs:
        copy.start()

    barrier = pltpu.get_barrier_semaphore()
    for step in range(1, span):
        pl.semaphore_signal(
            barrier, inc=1, device_id={"gx": lax.rem(x + gx - step, gx)},
            device_id_type=pl.DeviceIdType.MESH)

    @pl.when(has_left)
    def _():
        pl.semaphore_signal(
            barrier, inc=1, device_id={"gy": y - 1}, device_id_type=pl.DeviceIdType.MESH)

    @pl.when(has_right)
    def _():
        pl.semaphore_signal(
            barrier, inc=1, device_id={"gy": y + 1}, device_id_type=pl.DeviceIdType.MESH)

    for copy in inputs[:3]:
        copy.wait()
    row_id = lax.broadcasted_iota(jnp.int32, (rows, LANES), 0)
    lane_id = lax.broadcasted_iota(jnp.int32, (rows, LANES), 1)
    filled = jnp.zeros((rows, LANES), jnp.int32)
    for row in range(rows):
        entries = [a_cols_ref[k, row] for k in range(A_TILES)]
        entries += [new_row_ref[row]]
        entries += [p_cols_ref[q, row] for q in range(P_TILES)]
        for lane, entry in enumerate(entries):
            filled = jnp.where((row_id == row) & (lane_id == lane), entry, filled)
    table[...] = filled
    table_from[0] = filled
    table_ext[1] = filled

    def put_row(step, rank, target):
        owner = lax.rem(x + step, gx)
        row, _ = find_row(lambda r: new_row_ref[r], rows, per_owner, owner, rank)
        target[step, rank] = a_ref[row]

    def a_copy(step, rank):
        return pltpu.make_async_remote_copy(
            stage.at[step, rank], recv.at[step, rank],
            a_send.at[step, rank], a_recv.at[step, rank],
            device_id={"gx": lax.rem(x + step, gx)}, device_id_type=pl.DeviceIdType.MESH)

    def table_copy(step):
        return pltpu.make_async_remote_copy(
            table, table_from.at[step], t_send.at[step], t_recv.at[step],
            device_id={"gx": lax.rem(x + step, gx)}, device_id_type=pl.DeviceIdType.MESH)

    def halo_copies(side):
        target = y + 1 if side == 0 else y - 1
        place = 0 if side == 0 else 2
        return (
            pltpu.make_async_remote_copy(
                table, table_ext.at[place], ht_send.at[side], ht_recv.at[side],
                device_id={"gy": target}, device_id_type=pl.DeviceIdType.MESH),
            pltpu.make_async_remote_copy(
                p_hbm, ext.at[side], h_send.at[side], h_recv.at[side],
                device_id={"gy": target}, device_id_type=pl.DeviceIdType.MESH),
        )

    if gx == 4 and span == 4:
        odd = lax.rem(x, 2)
        send_order = [2, 3 - 2 * odd, 1 + 2 * odd]

        def arrival(n):
            later = n // 2
            return 2 * n * (1 - later) + later * (
                (1 - odd) * (3 - 2 * (n - 2)) + odd * (1 + 2 * (n - 2)))
    else:
        send_order = list(range(1, span))

        def arrival(n):
            return n

    for copy in inputs[3:]:
        copy.wait()
    put_row(send_order[0], 0, stage)
    greeted = span - 1 + jnp.where(has_left, 1, 0) + jnp.where(has_right, 1, 0)
    pl.semaphore_wait(barrier, greeted)
    def send_row(step, rank):
        if paced and step is send_order[1]:
            @pl.when(jnp.logical_not(first_core))
            def _():
                a_copy(step, rank).start()
        else:
            a_copy(step, rank).start()

    send_row(send_order[0], 0)
    put_row(send_order[0], 1, stage)
    send_row(send_order[0], 1)
    for step in range(1, span):
        table_copy(step).start()

    @pl.when(has_right)
    def _():
        for copy in halo_copies(0):
            copy.start()

    @pl.when(has_left)
    def _():
        for copy in halo_copies(1):
            copy.start()

    for step in send_order[1:]:
        for rank in range(CAP):
            put_row(step, rank, stage)
            send_row(step, rank)
    for rank in range(CAP):
        put_row(0, rank, recv)

    def split_p(source, base):
        def body(row, carry):
            for q in range(P_TILES):
                high, low = split(source[row, q])
                columns = pl.ds(q * tile, tile)
                ext_cat[base + row, pl.ds(0, tile), columns] = high
                ext_cat[base + row, pl.ds(tile, tile), columns] = high
                ext_cat[base + row, pl.ds(2 * tile, tile), columns] = low
            return carry
        lax.fori_loop(0, rows, body, 0)

    def flip(row, carry):
        for q in range(P_TILES):
            flipped[row, q] = p_ref[row, q].T
        return carry

    lax.fori_loop(0, rows, flip, 0)
    split_p(p_ref, rows)

    def clear(n, carry):
        for t in range(coarse):
            own_ref[t, n] = jnp.zeros((tile, tile), jnp.float32)
            following[t, n] = jnp.zeros((tile, tile), jnp.float32)
        return carry

    lax.fori_loop(0, 4 * coarse, clear, 0)

    @pl.when(jnp.logical_not(has_left))
    def _():
        copy = pltpu.make_async_copy(following, arrived_ref, local_sem.at[0])
        copy.start()
        copy.wait()

    for step in range(1, span):
        table_copy(step).wait_recv()

    @pl.when(has_left)
    def _():
        for copy in halo_copies(0):
            copy.wait_recv()
        split_p(ext.at[0], 0)

    @pl.when(jnp.logical_not(has_left))
    def _():
        table_ext[0] = jnp.zeros((rows, LANES), jnp.int32)

    @pl.when(has_right)
    def _():
        for copy in halo_copies(1):
            copy.wait_recv()
        split_p(ext.at[1], 2 * rows)

    @pl.when(jnp.logical_not(has_right))
    def _():
        table_ext[2] = jnp.zeros((rows, LANES), jnp.int32)

    to_scalar = (
        pltpu.make_async_copy(table_from, from_s, local_sem.at[0]),
        pltpu.make_async_copy(table_ext, ext_s, local_sem.at[1]),
    )
    for copy in to_scalar:
        copy.start()
    for copy in to_scalar:
        copy.wait()

    def next_copy(n):
        piece = pl.ds(2 * n, 2)
        return pltpu.make_async_remote_copy(
            following.at[:, piece], arrived_ref.at[:, piece], n_send.at[n], n_recv.at[n],
            device_id={"gy": y + 1}, device_id_type=pl.DeviceIdType.MESH)

    def one_distance(n, carry):
        step = arrival(n)
        if paced:
            @pl.when((n == 1) & first_core)
            def _():
                for rank in range(CAP):
                    a_copy(send_order[0], rank).wait_send()
                    a_copy(send_order[1], rank).start()

        slots = []
        lifts = [[] for _ in range(2 * coarse)]
        for rank in range(CAP):
            row, there = find_row(
                lambda r: from_s[step, r, ROW_LANE], rows, per_owner, x, rank)
            own_row = lax.rem(from_s[step, row, ROW_LANE], jnp.int32(rows))
            goals = [
                ext_s[1, own_row, P_LANE + p] - device * coarse for p in range(P_TILES)]
            for t in range(2 * coarse):
                lifts[t].append(sum(
                    jnp.where(goals[p] == t, 1.0, 0.0) * flipped[own_row, p]
                    for p in range(P_TILES)))
            wide, columns = [], []
            for k in range(A_TILES):
                column = jnp.where(there, from_s[step, row, k] - (device - 1) * rows, rows)
                column = jnp.minimum(jnp.maximum(column, 0), 3 * rows - 1)
                columns.append(column)
                for q in range(P_TILES):
                    goal = ext_s[lax.div(column, rows), lax.rem(column, rows), P_LANE + q]
                    wide.append(jnp.where(there, goal - (device - 1) * coarse, -1))

            @pl.when(n > 0)
            def _():
                a_copy(step, rank).wait_recv()

            slots.append(wide)
            for k in range(A_TILES):
                high, low = split(recv[step, rank, k])
                left = jnp.concatenate([high, low, high], axis=1)
                products[rank, k] = jnp.dot(
                    left, ext_cat[columns[k]], preferred_element_type=jnp.float32)

        lift_cat = []
        for t in range(2 * coarse):
            high, low = split(jnp.concatenate(lifts[t], axis=1))
            lift_cat.append(jnp.concatenate([high, low, high], axis=1))
        lift_cat = jnp.concatenate(lift_cat, axis=0)

        for c in range(chunks):
            halves = []
            for q in range(2):
                w = 2 * c + q
                parts = []
                for rank in range(CAP):
                    total = None
                    for m in range(A_TILES * P_TILES):
                        k, p = m // P_TILES, m % P_TILES
                        if not may_reach(k, p, w // coarse):
                            continue
                        weight = jnp.where(slots[rank][m] == w, 1.0, 0.0)
                        term = weight * products[rank, k, :, pl.ds(p * tile, tile)]
                        total = term if total is None else total + term
                    parts.append(total)
                high, low = split(jnp.concatenate(parts, axis=0))
                halves.append(jnp.concatenate([high, high, low], axis=0))
            right = jnp.concatenate(halves, axis=1)
            result = jnp.dot(lift_cat, right, preferred_element_type=jnp.float32)
            for t in range(2 * coarse):
                for q in range(2):
                    value = result[t * tile:(t + 1) * tile, q * tile:(q + 1) * tile]
                    if t < coarse:
                        own_ref[t, 2 * c + q] += value
                    else:
                        following[t - coarse, 2 * c + q] += value

            @pl.when((n == span - 1) & has_right)
            def _():
                next_copy(c).start()

        return carry

    lax.fori_loop(0, span, one_distance, 0)

    for step in range(1, span):
        table_copy(step).wait_send()
    for step in send_order:
        for rank in range(CAP):
            if paced and step is send_order[0]:
                @pl.when(jnp.logical_not(first_core))
                def _():
                    a_copy(step, rank).wait_send()
            else:
                a_copy(step, rank).wait_send()

    @pl.when(has_right)
    def _():
        for copy in halo_copies(0):
            copy.wait_send()
        for c in range(chunks):
            next_copy(c).wait_send()

    @pl.when(has_left)
    def _():
        for copy in halo_copies(1):
            copy.wait_send()
        for c in range(chunks):
            next_copy(c).wait_recv()


def shards(a_tiles, a_cols, new_row, p_tiles, p_cols):
    rows, tile = a_tiles.shape[0], a_tiles.shape[2]
    gx, gy = lax.axis_size("gx"), lax.axis_size("gy")
    span = min(SPAN, gx)
    coarse = rows // 4
    band = jax.ShapeDtypeStruct((coarse, 4 * coarse, tile, tile), jnp.float32)
    band_in = pltpu.VMEM(band.shape, jnp.float32)
    dma = pltpu.SemaphoreType.DMA
    row_block = (span, CAP, A_TILES, tile, tile)
    operands = [
        pltpu.with_memory_space_constraint(value, pltpu.HBM)
        for value in (new_row, a_cols.T, p_cols.T, a_tiles, p_tiles)]
    own, arrived = pl.pallas_call(
        functools.partial(kernel, span, gx, gy),
        out_shape=[band_in, band_in],
        in_specs=[pl.BlockSpec(memory_space=pl.ANY)] * 5,
        out_specs=[pl.BlockSpec(memory_space=pltpu.VMEM)] * 2,
        scratch_shapes=[
            pltpu.SMEM((rows,), jnp.int32),
            pltpu.SMEM((A_TILES, rows), jnp.int32),
            pltpu.SMEM((P_TILES, rows), jnp.int32),
            pltpu.VMEM(a_tiles.shape, jnp.float32),
            pltpu.VMEM(p_tiles.shape, jnp.float32),
            pltpu.VMEM(row_block, jnp.float32),
            pltpu.VMEM(row_block, jnp.float32),
            pltpu.VMEM((2, rows, P_TILES, tile, tile), jnp.float32),
            pltpu.VMEM((3 * rows, 3 * tile, P_TILES * tile), jnp.bfloat16),
            pltpu.VMEM((rows, P_TILES, tile, tile), jnp.float32),
            pltpu.VMEM((CAP, A_TILES, tile, P_TILES * tile), jnp.float32),
            pltpu.VMEM((coarse, 4 * coarse, tile, tile), jnp.float32),
            pltpu.VMEM((rows, LANES), jnp.int32),
            pltpu.VMEM((span, rows, LANES), jnp.int32),
            pltpu.VMEM((3, rows, LANES), jnp.int32),
            pltpu.SMEM((span, rows, LANES), jnp.int32),
            pltpu.SMEM((3, rows, LANES), jnp.int32),
            dma((span, CAP)), dma((span, CAP)), dma((span,)), dma((span,)),
            dma((2,)), dma((2,)), dma((2,)), dma((2,)),
            dma((2 * coarse,)), dma((2 * coarse,)), dma((5,)),
        ],
        compiler_params=pltpu.CompilerParams(
            collective_id=0, has_side_effects=True, vmem_limit_bytes=48 * 1024 * 1024),
        name="galerkin",
    )(*operands)
    pad = ((0, 0), (coarse, 0), (0, 0), (0, 0))
    behind = ((0, 0), (0, coarse), (0, 0), (0, 0))
    return jnp.pad(own, pad) + jnp.pad(arrived, behind)


def solution(mesh):
    in_specs = (
        P(("gx", "gy"), None, None, None),
        P(("gx", "gy"), None),
        P(("gx", "gy")),
        P(("gx", "gy"), None, None, None),
        P(("gx", "gy"), None),
    )
    out_specs = P(("gx", "gy"), None, None, None)
    return jax.shard_map(shards, mesh=mesh, in_specs=in_specs, out_specs=out_specs, check_vma=False)
```

```python
import functools

import jax
import jax.numpy as jnp
from jax import lax
from jax.experimental import pallas as pl
from jax.experimental.pallas import tpu as pltpu
from jax.sharding import PartitionSpec as P

A_TILES = 4
P_TILES = 2
CAP = 2
SPAN = 6
LANES = 128
ROW_LANE = A_TILES
P_LANE = A_TILES + 1


def split(value):
    high = value.astype(jnp.bfloat16)
    low = (value - high.astype(jnp.float32)).astype(jnp.bfloat16)
    return high, low


def find_row(new_row_of, rows, per_owner, owner, rank):
    seen = jnp.int32(0)
    found = jnp.int32(0)
    for row in range(rows):
        here = lax.div(new_row_of(row), jnp.int32(per_owner)) == owner
        found = jnp.where(here & (seen == rank), row, found)
        seen = seen + here.astype(jnp.int32)
    return found, seen > rank


def may_reach(k, p, place):
    columns = (1,) if k == 0 else (0, 1, 2)
    if p == 0:
        return place in columns
    return place - 1 in columns or place == 1


def kernel(
    span, gx, gy,
    new_row_hbm, a_cols_hbm, p_cols_hbm, a_hbm, p_hbm,
    own_ref, arrived_ref,
    new_row_ref, a_cols_ref, p_cols_ref, a_ref, p_ref,
    stage, recv, ext, ext_cat, flipped, products, following,
    table, table_from, table_ext, from_s, ext_s,
    a_send, a_recv, t_send, t_recv, h_send, h_recv, ht_send, ht_recv, n_send, n_recv, local_sem, gate,
):
    rows, tile = p_ref.shape[0], p_ref.shape[2]
    coarse = rows // 4
    chunks = 4 * coarse // 2
    x, y = lax.axis_index("gx"), lax.axis_index("gy")
    device = x * gy + y
    per_owner = rows * gy
    has_left, has_right = y > 0, y < gy - 1
    gated = gx == 4 and span == 4 and gy % 2 == 0
    first_core = lax.rem(y, 2) == 0

    inputs = [
        pltpu.make_async_copy(source, target, local_sem.at[n])
        for n, (source, target) in enumerate((
            (new_row_hbm, new_row_ref), (a_cols_hbm, a_cols_ref), (p_cols_hbm, p_cols_ref),
            (a_hbm, a_ref), (p_hbm, p_ref)))]
    for copy in inputs:
        copy.start()

    barrier = pltpu.get_barrier_semaphore()
    for step in range(1, span):
        pl.semaphore_signal(
            barrier, inc=1, device_id={"gx": lax.rem(x + gx - step, gx)},
            device_id_type=pl.DeviceIdType.MESH)

    @pl.when(has_left)
    def _():
        pl.semaphore_signal(
            barrier, inc=1, device_id={"gy": y - 1}, device_id_type=pl.DeviceIdType.MESH)

    @pl.when(has_right)
    def _():
        pl.semaphore_signal(
            barrier, inc=1, device_id={"gy": y + 1}, device_id_type=pl.DeviceIdType.MESH)

    for copy in inputs[:3]:
        copy.wait()
    row_id = lax.broadcasted_iota(jnp.int32, (rows, LANES), 0)
    lane_id = lax.broadcasted_iota(jnp.int32, (rows, LANES), 1)
    filled = jnp.zeros((rows, LANES), jnp.int32)
    for row in range(rows):
        entries = [a_cols_ref[k, row] for k in range(A_TILES)]
        entries += [new_row_ref[row]]
        entries += [p_cols_ref[q, row] for q in range(P_TILES)]
        for lane, entry in enumerate(entries):
            filled = jnp.where((row_id == row) & (lane_id == lane), entry, filled)
    table[...] = filled
    table_from[0] = filled
    table_ext[1] = filled

    def put_rows(step, target, slot):
        owner = lax.rem(x + step, gx)
        for rank in range(CAP):
            row, _ = find_row(lambda r: new_row_ref[r], rows, per_owner, owner, rank)
            target[slot, rank] = a_ref[row]

    def a_copy(step):
        return pltpu.make_async_remote_copy(
            stage.at[step], recv.at[step], a_send.at[step], a_recv.at[step],
            device_id={"gx": lax.rem(x + step, gx)}, device_id_type=pl.DeviceIdType.MESH)

    def table_copy(step):
        return pltpu.make_async_remote_copy(
            table, table_from.at[step], t_send.at[step], t_recv.at[step],
            device_id={"gx": lax.rem(x + step, gx)}, device_id_type=pl.DeviceIdType.MESH)

    def halo_copies(side):
        target = y + 1 if side == 0 else y - 1
        place = 0 if side == 0 else 2
        return (
            pltpu.make_async_remote_copy(
                table, table_ext.at[place], ht_send.at[side], ht_recv.at[side],
                device_id={"gy": target}, device_id_type=pl.DeviceIdType.MESH),
            pltpu.make_async_remote_copy(
                p_hbm, ext.at[side], h_send.at[side], h_recv.at[side],
                device_id={"gy": target}, device_id_type=pl.DeviceIdType.MESH),
        )

    if gx == 4 and span == 4:
        odd = lax.rem(x, 2)
        send_order = [2, 3 - 2 * odd, 1 + 2 * odd]

        def arrival(n):
            later = n // 2
            return 2 * n * (1 - later) + later * (
                (1 - odd) * (3 - 2 * (n - 2)) + odd * (1 + 2 * (n - 2)))
    else:
        send_order = list(range(1, span))

        def arrival(n):
            return n

    for copy in inputs[3:]:
        copy.wait()
    put_rows(send_order[0], stage, send_order[0])
    greeted = span - 1 + jnp.where(has_left, 1, 0) + jnp.where(has_right, 1, 0)
    pl.semaphore_wait(barrier, greeted)
    a_copy(send_order[0]).start()
    for step in range(1, span):
        table_copy(step).start()

    @pl.when(has_right)
    def _():
        for copy in halo_copies(0):
            copy.start()

    @pl.when(has_left)
    def _():
        for copy in halo_copies(1):
            copy.start()

    for n, step in enumerate(send_order[1:]):
        put_rows(step, stage, step)
        if gated and n == 0:
            @pl.when(jnp.logical_not(first_core))
            def _():
                a_copy(step).start()
        else:
            a_copy(step).start()
    put_rows(0, recv, 0)

    def split_p(source, base):
        def body(row, carry):
            for q in range(P_TILES):
                high, low = split(source[row, q])
                columns = pl.ds(q * tile, tile)
                ext_cat[base + row, pl.ds(0, tile), columns] = high
                ext_cat[base + row, pl.ds(tile, tile), columns] = high
                ext_cat[base + row, pl.ds(2 * tile, tile), columns] = low
            return carry
        lax.fori_loop(0, rows, body, 0)

    def flip(row, carry):
        for q in range(P_TILES):
            flipped[row, q] = p_ref[row, q].T
        return carry

    lax.fori_loop(0, rows, flip, 0)
    split_p(p_ref, rows)

    def clear(n, carry):
        for t in range(coarse):
            own_ref[t, n] = jnp.zeros((tile, tile), jnp.float32)
            following[t, n] = jnp.zeros((tile, tile), jnp.float32)
        return carry

    lax.fori_loop(0, 4 * coarse, clear, 0)

    @pl.when(jnp.logical_not(has_left))
    def _():
        copy = pltpu.make_async_copy(following, arrived_ref, local_sem.at[0])
        copy.start()
        copy.wait()

    for step in range(1, span):
        table_copy(step).wait_recv()

    @pl.when(has_left)
    def _():
        for copy in halo_copies(0):
            copy.wait_recv()
        split_p(ext.at[0], 0)

    @pl.when(jnp.logical_not(has_left))
    def _():
        table_ext[0] = jnp.zeros((rows, LANES), jnp.int32)

    @pl.when(has_right)
    def _():
        for copy in halo_copies(1):
            copy.wait_recv()
        split_p(ext.at[1], 2 * rows)

    @pl.when(jnp.logical_not(has_right))
    def _():
        table_ext[2] = jnp.zeros((rows, LANES), jnp.int32)

    to_scalar = (
        pltpu.make_async_copy(table_from, from_s, local_sem.at[0]),
        pltpu.make_async_copy(table_ext, ext_s, local_sem.at[1]),
    )
    for copy in to_scalar:
        copy.start()
    for copy in to_scalar:
        copy.wait()

    def next_copy(n):
        piece = pl.ds(2 * n, 2)
        return pltpu.make_async_remote_copy(
            following.at[:, piece], arrived_ref.at[:, piece], n_send.at[n], n_recv.at[n],
            device_id={"gy": y + 1}, device_id_type=pl.DeviceIdType.MESH)

    def one_distance(n, carry):
        step = arrival(n)
        if gated:
            @pl.when((n == 1) & first_core)
            def _():
                pl.semaphore_wait(gate, 1)
                a_copy(send_order[1]).start()

            @pl.when((n == 1) & jnp.logical_not(first_core))
            def _():
                for sent in send_order[:2]:
                    a_copy(sent).wait_send()
                pl.semaphore_signal(
                    gate, inc=1, device_id={"gy": y - 1}, device_id_type=pl.DeviceIdType.MESH)

        @pl.when(n > 0)
        def _():
            a_copy(step).wait_recv()

        slots = []
        lifts = [[] for _ in range(2 * coarse)]
        for rank in range(CAP):
            row, there = find_row(
                lambda r: from_s[step, r, ROW_LANE], rows, per_owner, x, rank)
            own_row = lax.rem(from_s[step, row, ROW_LANE], jnp.int32(rows))
            wide = []
            for k in range(A_TILES):
                column = jnp.where(there, from_s[step, row, k] - (device - 1) * rows, rows)
                column = jnp.minimum(jnp.maximum(column, 0), 3 * rows - 1)
                for q in range(P_TILES):
                    goal = ext_s[lax.div(column, rows), lax.rem(column, rows), P_LANE + q]
                    wide.append(jnp.where(there, goal - (device - 1) * coarse, -1))
                high, low = split(recv[step, rank, k])
                left = jnp.concatenate([high, low, high], axis=1)
                products[rank, k] = jnp.dot(
                    left, ext_cat[column], preferred_element_type=jnp.float32)
            slots.append(wide)
            goals = [
                ext_s[1, own_row, P_LANE + p] - device * coarse for p in range(P_TILES)]
            for t in range(2 * coarse):
                lifts[t].append(sum(
                    jnp.where(goals[p] == t, 1.0, 0.0) * flipped[own_row, p]
                    for p in range(P_TILES)))
        lift_cat = []
        for t in range(2 * coarse):
            high, low = split(jnp.concatenate(lifts[t], axis=1))
            lift_cat.append(jnp.concatenate([high, low, high], axis=1))
        lift_cat = jnp.concatenate(lift_cat, axis=0)

        for c in range(chunks):
            halves = []
            for q in range(2):
                w = 2 * c + q
                parts = []
                for rank in range(CAP):
                    total = None
                    for m in range(A_TILES * P_TILES):
                        k, p = m // P_TILES, m % P_TILES
                        if not may_reach(k, p, w // coarse):
                            continue
                        weight = jnp.where(slots[rank][m] == w, 1.0, 0.0)
                        term = weight * products[rank, k, :, pl.ds(p * tile, tile)]
                        total = term if total is None else total + term
                    parts.append(total)
                high, low = split(jnp.concatenate(parts, axis=0))
                halves.append(jnp.concatenate([high, high, low], axis=0))
            right = jnp.concatenate(halves, axis=1)
            result = jnp.dot(lift_cat, right, preferred_element_type=jnp.float32)
            for t in range(2 * coarse):
                for q in range(2):
                    value = result[t * tile:(t + 1) * tile, q * tile:(q + 1) * tile]
                    if t < coarse:
                        own_ref[t, 2 * c + q] += value
                    else:
                        following[t - coarse, 2 * c + q] += value

            @pl.when((n == span - 1) & has_right)
            def _():
                next_copy(c).start()

        return carry

    lax.fori_loop(0, span, one_distance, 0)

    for step in range(1, span):
        table_copy(step).wait_send()
    if gated:
        @pl.when(first_core)
        def _():
            for step in send_order[:2]:
                a_copy(step).wait_send()

        a_copy(send_order[2]).wait_send()
    else:
        for step in send_order:
            a_copy(step).wait_send()

    @pl.when(has_right)
    def _():
        for copy in halo_copies(0):
            copy.wait_send()
        for c in range(chunks):
            next_copy(c).wait_send()

    @pl.when(has_left)
    def _():
        for copy in halo_copies(1):
            copy.wait_send()
        for c in range(chunks):
            next_copy(c).wait_recv()


def shards(a_tiles, a_cols, new_row, p_tiles, p_cols):
    rows, tile = a_tiles.shape[0], a_tiles.shape[2]
    gx, gy = lax.axis_size("gx"), lax.axis_size("gy")
    span = min(SPAN, gx)
    coarse = rows // 4
    band = jax.ShapeDtypeStruct((coarse, 4 * coarse, tile, tile), jnp.float32)
    band_in = pltpu.VMEM(band.shape, jnp.float32)
    dma = pltpu.SemaphoreType.DMA
    row_block = (span, CAP, A_TILES, tile, tile)
    operands = [
        pltpu.with_memory_space_constraint(value, pltpu.HBM)
        for value in (new_row, a_cols.T, p_cols.T, a_tiles, p_tiles)]
    own, arrived = pl.pallas_call(
        functools.partial(kernel, span, gx, gy),
        out_shape=[band_in, band_in],
        in_specs=[pl.BlockSpec(memory_space=pl.ANY)] * 5,
        out_specs=[pl.BlockSpec(memory_space=pltpu.VMEM)] * 2,
        scratch_shapes=[
            pltpu.SMEM((rows,), jnp.int32),
            pltpu.SMEM((A_TILES, rows), jnp.int32),
            pltpu.SMEM((P_TILES, rows), jnp.int32),
            pltpu.VMEM(a_tiles.shape, jnp.float32),
            pltpu.VMEM(p_tiles.shape, jnp.float32),
            pltpu.VMEM(row_block, jnp.float32),
            pltpu.VMEM(row_block, jnp.float32),
            pltpu.VMEM((2, rows, P_TILES, tile, tile), jnp.float32),
            pltpu.VMEM((3 * rows, 3 * tile, P_TILES * tile), jnp.bfloat16),
            pltpu.VMEM((rows, P_TILES, tile, tile), jnp.float32),
            pltpu.VMEM((CAP, A_TILES, tile, P_TILES * tile), jnp.float32),
            pltpu.VMEM((coarse, 4 * coarse, tile, tile), jnp.float32),
            pltpu.VMEM((rows, LANES), jnp.int32),
            pltpu.VMEM((span, rows, LANES), jnp.int32),
            pltpu.VMEM((3, rows, LANES), jnp.int32),
            pltpu.SMEM((span, rows, LANES), jnp.int32),
            pltpu.SMEM((3, rows, LANES), jnp.int32),
            dma((span,)), dma((span,)), dma((span,)), dma((span,)),
            dma((2,)), dma((2,)), dma((2,)), dma((2,)),
            dma((2 * coarse,)), dma((2 * coarse,)), dma((5,)),
            pltpu.SemaphoreType.REGULAR,
        ],
        compiler_params=pltpu.CompilerParams(
            collective_id=0, has_side_effects=True, vmem_limit_bytes=48 * 1024 * 1024),
        name="galerkin",
    )(*operands)
    pad = ((0, 0), (coarse, 0), (0, 0), (0, 0))
    behind = ((0, 0), (0, coarse), (0, 0), (0, 0))
    return jnp.pad(own, pad) + jnp.pad(arrived, behind)


def solution(mesh):
    in_specs = (
        P(("gx", "gy"), None, None, None),
        P(("gx", "gy"), None),
        P(("gx", "gy")),
        P(("gx", "gy"), None, None, None),
        P(("gx", "gy"), None),
    )
    out_specs = P(("gx", "gy"), None, None, None)
    return jax.shard_map(shards, mesh=mesh, in_specs=in_specs, out_specs=out_specs, check_vma=False)
```

```python
import functools

import jax
import jax.numpy as jnp
from jax import lax
from jax.experimental import pallas as pl
from jax.experimental.pallas import tpu as pltpu
from jax.sharding import PartitionSpec as P

A_TILES = 4
P_TILES = 2
CAP = 2
SPAN = 6
LANES = 128
ROW_LANE = A_TILES
P_LANE = A_TILES + 1


def split(value):
    high = value.astype(jnp.bfloat16)
    low = (value - high.astype(jnp.float32)).astype(jnp.bfloat16)
    return high, low


def find_row(new_row_of, rows, per_owner, owner, rank):
    seen = jnp.int32(0)
    found = jnp.int32(0)
    for row in range(rows):
        here = lax.div(new_row_of(row), jnp.int32(per_owner)) == owner
        found = jnp.where(here & (seen == rank), row, found)
        seen = seen + here.astype(jnp.int32)
    return found, seen > rank


def may_reach(k, p, place):
    columns = (1,) if k == 0 else (0, 1, 2)
    if p == 0:
        return place in columns
    return place - 1 in columns or place == 1


def kernel(
    span, gx, gy,
    new_row_hbm, a_cols_hbm, p_cols_hbm, a_hbm, p_hbm,
    own_ref, arrived_ref,
    new_row_ref, a_cols_ref, p_cols_ref, a_ref, p_ref,
    stage, recv, ext, ext_cat, flipped, products, following,
    table, table_from, table_ext, from_s, ext_s,
    a_send, a_recv, t_send, t_recv, h_send, h_recv, ht_send, ht_recv, n_send, n_recv, local_sem, gate,
):
    rows, tile = p_ref.shape[0], p_ref.shape[2]
    coarse = rows // 4
    chunks = 4 * coarse // 2
    x, y = lax.axis_index("gx"), lax.axis_index("gy")
    device = x * gy + y
    per_owner = rows * gy
    has_left, has_right = y > 0, y < gy - 1
    gated = gx == 4 and span == 4 and gy % 2 == 0
    first_core = lax.rem(y, 2) == 0

    inputs = [
        pltpu.make_async_copy(source, target, local_sem.at[n])
        for n, (source, target) in enumerate((
            (a_hbm, a_ref), (new_row_hbm, new_row_ref), (a_cols_hbm, a_cols_ref),
            (p_cols_hbm, p_cols_ref), (p_hbm, p_ref)))]
    for copy in inputs:
        copy.start()

    barrier = pltpu.get_barrier_semaphore()
    for step in range(1, span):
        pl.semaphore_signal(
            barrier, inc=1, device_id={"gx": lax.rem(x + gx - step, gx)},
            device_id_type=pl.DeviceIdType.MESH)

    @pl.when(has_left)
    def _():
        pl.semaphore_signal(
            barrier, inc=1, device_id={"gy": y - 1}, device_id_type=pl.DeviceIdType.MESH)

    @pl.when(has_right)
    def _():
        pl.semaphore_signal(
            barrier, inc=1, device_id={"gy": y + 1}, device_id_type=pl.DeviceIdType.MESH)

    for copy in inputs[1:4]:
        copy.wait()
    row_id = lax.broadcasted_iota(jnp.int32, (rows, LANES), 0)
    lane_id = lax.broadcasted_iota(jnp.int32, (rows, LANES), 1)
    filled = jnp.zeros((rows, LANES), jnp.int32)
    for row in range(rows):
        entries = [a_cols_ref[k, row] for k in range(A_TILES)]
        entries += [new_row_ref[row]]
        entries += [p_cols_ref[q, row] for q in range(P_TILES)]
        for lane, entry in enumerate(entries):
            filled = jnp.where((row_id == row) & (lane_id == lane), entry, filled)
    table[...] = filled
    table_from[0] = filled
    table_ext[1] = filled

    def put_rows(step, target, slot):
        owner = lax.rem(x + step, gx)
        for rank in range(CAP):
            row, _ = find_row(lambda r: new_row_ref[r], rows, per_owner, owner, rank)
            target[slot, rank] = a_ref[row]

    def a_copy(step):
        return pltpu.make_async_remote_copy(
            stage.at[step], recv.at[step], a_send.at[step], a_recv.at[step],
            device_id={"gx": lax.rem(x + step, gx)}, device_id_type=pl.DeviceIdType.MESH)

    def table_copy(step):
        return pltpu.make_async_remote_copy(
            table, table_from.at[step], t_send.at[step], t_recv.at[step],
            device_id={"gx": lax.rem(x + step, gx)}, device_id_type=pl.DeviceIdType.MESH)

    def halo_copies(side):
        target = y + 1 if side == 0 else y - 1
        place = 0 if side == 0 else 2
        return (
            pltpu.make_async_remote_copy(
                table, table_ext.at[place], ht_send.at[side], ht_recv.at[side],
                device_id={"gy": target}, device_id_type=pl.DeviceIdType.MESH),
            pltpu.make_async_remote_copy(
                p_hbm, ext.at[side], h_send.at[side], h_recv.at[side],
                device_id={"gy": target}, device_id_type=pl.DeviceIdType.MESH),
        )

    if gx == 4 and span == 4:
        odd = lax.rem(x, 2)
        core = lax.rem(y, 2)
        beside = 1 + 2 * odd
        send_order = [2 * (1 - core) + beside * core, beside * (1 - core) + 2 * core, 4 - beside]
        came = 3 - 2 * odd
        came_order = [2 * (1 - core) + came * core, came * (1 - core) + 2 * core, 4 - came]

        def arrival(n):
            low, high = lax.rem(n, 2), n // 2
            return (came_order[0] * low * (1 - high) + came_order[1] * (1 - low) * high
                    + came_order[2] * low * high)
    else:
        send_order = list(range(1, span))

        def arrival(n):
            return n

    inputs[0].wait()
    put_rows(send_order[0], stage, send_order[0])
    greeted = span - 1 + jnp.where(has_left, 1, 0) + jnp.where(has_right, 1, 0)
    pl.semaphore_wait(barrier, greeted)
    a_copy(send_order[0]).start()
    for step in range(1, span):
        table_copy(step).start()

    @pl.when(has_right)
    def _():
        for copy in halo_copies(0):
            copy.start()

    @pl.when(has_left)
    def _():
        for copy in halo_copies(1):
            copy.start()

    for step in send_order[1:]:
        put_rows(step, stage, step)
        if gated and step is send_order[2]:
            @pl.when(jnp.logical_not(first_core))
            def _():
                a_copy(step).start()
        else:
            a_copy(step).start()
    put_rows(0, recv, 0)

    def split_p(source, base):
        def body(row, carry):
            for q in range(P_TILES):
                high, low = split(source[row, q])
                columns = pl.ds(q * tile, tile)
                ext_cat[base + row, pl.ds(0, tile), columns] = high
                ext_cat[base + row, pl.ds(tile, tile), columns] = high
                ext_cat[base + row, pl.ds(2 * tile, tile), columns] = low
            return carry
        lax.fori_loop(0, rows, body, 0)

    def flip(row, carry):
        for q in range(P_TILES):
            flipped[row, q] = p_ref[row, q].T
        return carry

    inputs[4].wait()
    lax.fori_loop(0, rows, flip, 0)
    split_p(p_ref, rows)

    def clear(n, carry):
        for t in range(coarse):
            own_ref[t, n] = jnp.zeros((tile, tile), jnp.float32)
            following[t, n] = jnp.zeros((tile, tile), jnp.float32)
        return carry

    lax.fori_loop(0, 4 * coarse, clear, 0)

    @pl.when(jnp.logical_not(has_left))
    def _():
        copy = pltpu.make_async_copy(following, arrived_ref, local_sem.at[0])
        copy.start()
        copy.wait()

    for step in range(1, span):
        table_copy(step).wait_recv()

    @pl.when(has_left)
    def _():
        for copy in halo_copies(0):
            copy.wait_recv()
        split_p(ext.at[0], 0)

    @pl.when(jnp.logical_not(has_left))
    def _():
        table_ext[0] = jnp.zeros((rows, LANES), jnp.int32)

    @pl.when(has_right)
    def _():
        for copy in halo_copies(1):
            copy.wait_recv()
        split_p(ext.at[1], 2 * rows)

    @pl.when(jnp.logical_not(has_right))
    def _():
        table_ext[2] = jnp.zeros((rows, LANES), jnp.int32)

    to_scalar = (
        pltpu.make_async_copy(table_from, from_s, local_sem.at[0]),
        pltpu.make_async_copy(table_ext, ext_s, local_sem.at[1]),
    )
    for copy in to_scalar:
        copy.start()
    for copy in to_scalar:
        copy.wait()

    def next_copy(n):
        piece = pl.ds(2 * n, 2)
        return pltpu.make_async_remote_copy(
            following.at[:, piece], arrived_ref.at[:, piece], n_send.at[n], n_recv.at[n],
            device_id={"gy": y + 1}, device_id_type=pl.DeviceIdType.MESH)

    def one_distance(n, carry):
        step = arrival(n)
        if gated:
            @pl.when((n == span - 1) & first_core)
            def _():
                pl.semaphore_wait(gate, 1)
                a_copy(send_order[2]).start()

            @pl.when((n == span - 1) & jnp.logical_not(first_core))
            def _():
                for sent in send_order[1:]:
                    a_copy(sent).wait_send()
                pl.semaphore_signal(
                    gate, inc=1, device_id={"gy": y - 1}, device_id_type=pl.DeviceIdType.MESH)

        @pl.when(n > 0)
        def _():
            a_copy(step).wait_recv()

        slots = []
        lifts = [[] for _ in range(2 * coarse)]
        for rank in range(CAP):
            row, there = find_row(
                lambda r: from_s[step, r, ROW_LANE], rows, per_owner, x, rank)
            own_row = lax.rem(from_s[step, row, ROW_LANE], jnp.int32(rows))
            wide = []
            for k in range(A_TILES):
                column = jnp.where(there, from_s[step, row, k] - (device - 1) * rows, rows)
                column = jnp.minimum(jnp.maximum(column, 0), 3 * rows - 1)
                for q in range(P_TILES):
                    goal = ext_s[lax.div(column, rows), lax.rem(column, rows), P_LANE + q]
                    wide.append(jnp.where(there, goal - (device - 1) * coarse, -1))
                high, low = split(recv[step, rank, k])
                left = jnp.concatenate([high, low, high], axis=1)
                products[rank, k] = jnp.dot(
                    left, ext_cat[column], preferred_element_type=jnp.float32)
            slots.append(wide)
            goals = [
                ext_s[1, own_row, P_LANE + p] - device * coarse for p in range(P_TILES)]
            for t in range(2 * coarse):
                lifts[t].append(sum(
                    jnp.where(goals[p] == t, 1.0, 0.0) * flipped[own_row, p]
                    for p in range(P_TILES)))
        lift_cat = []
        for t in range(2 * coarse):
            high, low = split(jnp.concatenate(lifts[t], axis=1))
            lift_cat.append(jnp.concatenate([high, low, high], axis=1))
        lift_cat = jnp.concatenate(lift_cat, axis=0)

        for c in range(chunks):
            halves = []
            for q in range(2):
                w = 2 * c + q
                parts = []
                for rank in range(CAP):
                    total = None
                    for m in range(A_TILES * P_TILES):
                        k, p = m // P_TILES, m % P_TILES
                        if not may_reach(k, p, w // coarse):
                            continue
                        weight = jnp.where(slots[rank][m] == w, 1.0, 0.0)
                        term = weight * products[rank, k, :, pl.ds(p * tile, tile)]
                        total = term if total is None else total + term
                    parts.append(total)
                high, low = split(jnp.concatenate(parts, axis=0))
                halves.append(jnp.concatenate([high, high, low], axis=0))
            right = jnp.concatenate(halves, axis=1)
            result = jnp.dot(lift_cat, right, preferred_element_type=jnp.float32)
            for t in range(2 * coarse):
                for q in range(2):
                    value = result[t * tile:(t + 1) * tile, q * tile:(q + 1) * tile]
                    if t < coarse:
                        own_ref[t, 2 * c + q] += value
                    else:
                        following[t - coarse, 2 * c + q] += value

            @pl.when((n == span - 1) & has_right)
            def _():
                next_copy(c).start()

        return carry

    lax.fori_loop(0, span, one_distance, 0)

    for step in range(1, span):
        table_copy(step).wait_send()
    a_copy(send_order[0]).wait_send()
    if gated:
        @pl.when(first_core)
        def _():
            for step in send_order[1:]:
                a_copy(step).wait_send()
    else:
        for step in send_order[1:]:
            a_copy(step).wait_send()

    @pl.when(has_right)
    def _():
        for copy in halo_copies(0):
            copy.wait_send()
        for c in range(chunks):
            next_copy(c).wait_send()

    @pl.when(has_left)
    def _():
        for copy in halo_copies(1):
            copy.wait_send()
        for c in range(chunks):
            next_copy(c).wait_recv()


def shards(a_tiles, a_cols, new_row, p_tiles, p_cols):
    rows, tile = a_tiles.shape[0], a_tiles.shape[2]
    gx, gy = lax.axis_size("gx"), lax.axis_size("gy")
    span = min(SPAN, gx)
    coarse = rows // 4
    band = jax.ShapeDtypeStruct((coarse, 4 * coarse, tile, tile), jnp.float32)
    band_in = pltpu.VMEM(band.shape, jnp.float32)
    dma = pltpu.SemaphoreType.DMA
    row_block = (span, CAP, A_TILES, tile, tile)
    operands = [
        pltpu.with_memory_space_constraint(value, pltpu.HBM)
        for value in (new_row, a_cols.T, p_cols.T, a_tiles, p_tiles)]
    own, arrived = pl.pallas_call(
        functools.partial(kernel, span, gx, gy),
        out_shape=[band_in, band_in],
        in_specs=[pl.BlockSpec(memory_space=pl.ANY)] * 5,
        out_specs=[pl.BlockSpec(memory_space=pltpu.VMEM)] * 2,
        scratch_shapes=[
            pltpu.SMEM((rows,), jnp.int32),
            pltpu.SMEM((A_TILES, rows), jnp.int32),
            pltpu.SMEM((P_TILES, rows), jnp.int32),
            pltpu.VMEM(a_tiles.shape, jnp.float32),
            pltpu.VMEM(p_tiles.shape, jnp.float32),
            pltpu.VMEM(row_block, jnp.float32),
            pltpu.VMEM(row_block, jnp.float32),
            pltpu.VMEM((2, rows, P_TILES, tile, tile), jnp.float32),
            pltpu.VMEM((3 * rows, 3 * tile, P_TILES * tile), jnp.bfloat16),
            pltpu.VMEM((rows, P_TILES, tile, tile), jnp.float32),
            pltpu.VMEM((CAP, A_TILES, tile, P_TILES * tile), jnp.float32),
            pltpu.VMEM((coarse, 4 * coarse, tile, tile), jnp.float32),
            pltpu.VMEM((rows, LANES), jnp.int32),
            pltpu.VMEM((span, rows, LANES), jnp.int32),
            pltpu.VMEM((3, rows, LANES), jnp.int32),
            pltpu.SMEM((span, rows, LANES), jnp.int32),
            pltpu.SMEM((3, rows, LANES), jnp.int32),
            dma((span,)), dma((span,)), dma((span,)), dma((span,)),
            dma((2,)), dma((2,)), dma((2,)), dma((2,)),
            dma((2 * coarse,)), dma((2 * coarse,)), dma((5,)),
            pltpu.SemaphoreType.REGULAR,
        ],
        compiler_params=pltpu.CompilerParams(
            collective_id=0, has_side_effects=True, vmem_limit_bytes=48 * 1024 * 1024),
        name="galerkin",
    )(*operands)
    pad = ((0, 0), (coarse, 0), (0, 0), (0, 0))
    behind = ((0, 0), (0, coarse), (0, 0), (0, 0))
    return jnp.pad(own, pad) + jnp.pad(arrived, behind)


def solution(mesh):
    in_specs = (
        P(("gx", "gy"), None, None, None),
        P(("gx", "gy"), None),
        P(("gx", "gy")),
        P(("gx", "gy"), None, None, None),
        P(("gx", "gy"), None),
    )
    out_specs = P(("gx", "gy"), None, None, None)
    return jax.shard_map(shards, mesh=mesh, in_specs=in_specs, out_specs=out_specs, check_vma=False)
```

```python
import functools

import jax
import jax.numpy as jnp
from jax import lax
from jax.experimental import pallas as pl
from jax.experimental.pallas import tpu as pltpu
from jax.sharding import PartitionSpec as P

A_TILES = 4
P_TILES = 2
CAP = 2
SPAN = 6
LANES = 128
ROW_LANE = A_TILES
P_LANE = A_TILES + 1


def split(value):
    high = value.astype(jnp.bfloat16)
    low = (value - high.astype(jnp.float32)).astype(jnp.bfloat16)
    return high, low


def find_row(new_row_of, rows, per_owner, owner, rank):
    seen = jnp.int32(0)
    found = jnp.int32(0)
    for row in range(rows):
        here = lax.div(new_row_of(row), jnp.int32(per_owner)) == owner
        found = jnp.where(here & (seen == rank), row, found)
        seen = seen + here.astype(jnp.int32)
    return found, seen > rank


def may_reach(k, p, place):
    columns = (1,) if k == 0 else (0, 1, 2)
    if p == 0:
        return place in columns
    return place - 1 in columns or place == 1


def kernel(
    span, gx, gy,
    new_row_hbm, a_cols_hbm, p_cols_hbm, a_hbm, p_hbm,
    own_ref, arrived_ref,
    new_row_ref, a_cols_ref, p_cols_ref, a_ref, p_ref,
    stage, recv, ext, ext_cat, flipped, products, following,
    table, table_from, table_ext, from_s, ext_s,
    a_send, a_recv, t_send, t_recv, h_send, h_recv, ht_send, ht_recv, n_send, n_recv, local_sem, gate,
):
    rows, tile = p_ref.shape[0], p_ref.shape[2]
    coarse = rows // 4
    chunks = 4 * coarse // 2
    x, y = lax.axis_index("gx"), lax.axis_index("gy")
    device = x * gy + y
    per_owner = rows * gy
    has_left, has_right = y > 0, y < gy - 1
    gated = gx == 4 and span == 4 and gy % 2 == 0
    first_core = lax.rem(y, 2) == 0

    inputs = [
        pltpu.make_async_copy(source, target, local_sem.at[n])
        for n, (source, target) in enumerate((
            (a_hbm, a_ref), (new_row_hbm, new_row_ref), (a_cols_hbm, a_cols_ref),
            (p_cols_hbm, p_cols_ref), (p_hbm, p_ref)))]
    for copy in inputs:
        copy.start()

    barrier = pltpu.get_barrier_semaphore()
    for step in range(1, span):
        pl.semaphore_signal(
            barrier, inc=1, device_id={"gx": lax.rem(x + gx - step, gx)},
            device_id_type=pl.DeviceIdType.MESH)

    @pl.when(has_left)
    def _():
        pl.semaphore_signal(
            barrier, inc=1, device_id={"gy": y - 1}, device_id_type=pl.DeviceIdType.MESH)

    @pl.when(has_right)
    def _():
        pl.semaphore_signal(
            barrier, inc=1, device_id={"gy": y + 1}, device_id_type=pl.DeviceIdType.MESH)

    for copy in inputs[1:4]:
        copy.wait()
    row_id = lax.broadcasted_iota(jnp.int32, (rows, LANES), 0)
    lane_id = lax.broadcasted_iota(jnp.int32, (rows, LANES), 1)
    filled = jnp.zeros((rows, LANES), jnp.int32)
    for row in range(rows):
        entries = [a_cols_ref[k, row] for k in range(A_TILES)]
        entries += [new_row_ref[row]]
        entries += [p_cols_ref[q, row] for q in range(P_TILES)]
        for lane, entry in enumerate(entries):
            filled = jnp.where((row_id == row) & (lane_id == lane), entry, filled)
    table[...] = filled
    table_from[0] = filled
    table_ext[1] = filled

    def put_rows(step, target, slot):
        owner = lax.rem(x + step, gx)
        for rank in range(CAP):
            row, _ = find_row(lambda r: new_row_ref[r], rows, per_owner, owner, rank)
            target[slot, rank] = a_ref[row]

    def a_copy(step):
        return pltpu.make_async_remote_copy(
            stage.at[step], recv.at[step], a_send.at[step], a_recv.at[step],
            device_id={"gx": lax.rem(x + step, gx)}, device_id_type=pl.DeviceIdType.MESH)

    def table_copy(step):
        return pltpu.make_async_remote_copy(
            table, table_from.at[step], t_send.at[step], t_recv.at[step],
            device_id={"gx": lax.rem(x + step, gx)}, device_id_type=pl.DeviceIdType.MESH)

    def halo_copies(side):
        target = y + 1 if side == 0 else y - 1
        place = 0 if side == 0 else 2
        return (
            pltpu.make_async_remote_copy(
                table, table_ext.at[place], ht_send.at[side], ht_recv.at[side],
                device_id={"gy": target}, device_id_type=pl.DeviceIdType.MESH),
            pltpu.make_async_remote_copy(
                p_hbm, ext.at[side], h_send.at[side], h_recv.at[side],
                device_id={"gy": target}, device_id_type=pl.DeviceIdType.MESH),
        )

    if gx == 4 and span == 4:
        odd = lax.rem(x, 2)
        core = lax.rem(y, 2)
        beside = 1 + 2 * odd
        send_order = [2 * (1 - core) + beside * core, beside * (1 - core) + 2 * core, 4 - beside]
        came = 3 - 2 * odd
        came_order = [2 * (1 - core) + came * core, came * (1 - core) + 2 * core, 4 - came]

        def arrival(n):
            low, high = lax.rem(n, 2), n // 2
            return (came_order[0] * low * (1 - high) + came_order[1] * (1 - low) * high
                    + came_order[2] * low * high)
    else:
        send_order = list(range(1, span))

        def arrival(n):
            return n

    inputs[0].wait()
    put_rows(send_order[0], stage, send_order[0])
    greeted = span - 1 + jnp.where(has_left, 1, 0) + jnp.where(has_right, 1, 0)
    pl.semaphore_wait(barrier, greeted)
    a_copy(send_order[0]).start()
    for step in range(1, span):
        table_copy(step).start()

    @pl.when(has_right)
    def _():
        for copy in halo_copies(0):
            copy.start()

    @pl.when(has_left)
    def _():
        for copy in halo_copies(1):
            copy.start()

    for step in send_order[1:]:
        put_rows(step, stage, step)
        if gated and step is send_order[2]:
            @pl.when(jnp.logical_not(first_core))
            def _():
                a_copy(step).start()
        else:
            a_copy(step).start()
    put_rows(0, recv, 0)

    def split_p(source, base):
        def body(row, carry):
            for q in range(P_TILES):
                high, low = split(source[row, q])
                columns = pl.ds(q * tile, tile)
                ext_cat[base + row, pl.ds(0, tile), columns] = high
                ext_cat[base + row, pl.ds(tile, tile), columns] = high
                ext_cat[base + row, pl.ds(2 * tile, tile), columns] = low
            return carry
        lax.fori_loop(0, rows, body, 0)

    def flip(row, carry):
        for q in range(P_TILES):
            flipped[row, q] = p_ref[row, q].T
        return carry

    inputs[4].wait()
    lax.fori_loop(0, rows, flip, 0)
    split_p(p_ref, rows)

    def clear(n, carry):
        for t in range(coarse):
            own_ref[t, n] = jnp.zeros((tile, tile), jnp.float32)
            following[t, n] = jnp.zeros((tile, tile), jnp.float32)
        return carry

    lax.fori_loop(0, 4 * coarse, clear, 0)

    @pl.when(jnp.logical_not(has_left))
    def _():
        copy = pltpu.make_async_copy(following, arrived_ref, local_sem.at[0])
        copy.start()
        copy.wait()

    for step in range(1, span):
        table_copy(step).wait_recv()

    @pl.when(has_left)
    def _():
        for copy in halo_copies(0):
            copy.wait_recv()
        split_p(ext.at[0], 0)

    @pl.when(jnp.logical_not(has_left))
    def _():
        table_ext[0] = jnp.zeros((rows, LANES), jnp.int32)

    @pl.when(has_right)
    def _():
        for copy in halo_copies(1):
            copy.wait_recv()
        split_p(ext.at[1], 2 * rows)

    @pl.when(jnp.logical_not(has_right))
    def _():
        table_ext[2] = jnp.zeros((rows, LANES), jnp.int32)

    to_scalar = (
        pltpu.make_async_copy(table_from, from_s, local_sem.at[0]),
        pltpu.make_async_copy(table_ext, ext_s, local_sem.at[1]),
    )
    for copy in to_scalar:
        copy.start()
    for copy in to_scalar:
        copy.wait()

    def next_copy(n):
        piece = pl.ds(2 * n, 2)
        return pltpu.make_async_remote_copy(
            following.at[:, piece], arrived_ref.at[:, piece], n_send.at[n], n_recv.at[n],
            device_id={"gy": y + 1}, device_id_type=pl.DeviceIdType.MESH)

    def one_distance(n, carry):
        step = arrival(n)
        if gated:
            @pl.when((n == 2) & first_core)
            def _():
                pl.semaphore_wait(gate, 1)
                a_copy(send_order[2]).start()

            @pl.when((n == 2) & jnp.logical_not(first_core))
            def _():
                for sent in send_order[1:]:
                    a_copy(sent).wait_send()
                pl.semaphore_signal(
                    gate, inc=1, device_id={"gy": y - 1}, device_id_type=pl.DeviceIdType.MESH)

        @pl.when(n > 0)
        def _():
            a_copy(step).wait_recv()

        slots = []
        lifts = [[] for _ in range(2 * coarse)]
        for rank in range(CAP):
            row, there = find_row(
                lambda r: from_s[step, r, ROW_LANE], rows, per_owner, x, rank)
            own_row = lax.rem(from_s[step, row, ROW_LANE], jnp.int32(rows))
            wide = []
            for k in range(A_TILES):
                column = jnp.where(there, from_s[step, row, k] - (device - 1) * rows, rows)
                column = jnp.minimum(jnp.maximum(column, 0), 3 * rows - 1)
                for q in range(P_TILES):
                    goal = ext_s[lax.div(column, rows), lax.rem(column, rows), P_LANE + q]
                    wide.append(jnp.where(there, goal - (device - 1) * coarse, -1))
                high, low = split(recv[step, rank, k])
                left = jnp.concatenate([high, low, high], axis=1)
                products[rank, k] = jnp.dot(
                    left, ext_cat[column], preferred_element_type=jnp.float32)
            slots.append(wide)
            goals = [
                ext_s[1, own_row, P_LANE + p] - device * coarse for p in range(P_TILES)]
            for t in range(2 * coarse):
                lifts[t].append(sum(
                    jnp.where(goals[p] == t, 1.0, 0.0) * flipped[own_row, p]
                    for p in range(P_TILES)))
        lift_cat = []
        for t in range(2 * coarse):
            high, low = split(jnp.concatenate(lifts[t], axis=1))
            lift_cat.append(jnp.concatenate([high, low, high], axis=1))
        lift_cat = jnp.concatenate(lift_cat, axis=0)

        for c in range(chunks):
            halves = []
            for q in range(2):
                w = 2 * c + q
                parts = []
                for rank in range(CAP):
                    total = None
                    for m in range(A_TILES * P_TILES):
                        k, p = m // P_TILES, m % P_TILES
                        if not may_reach(k, p, w // coarse):
                            continue
                        weight = jnp.where(slots[rank][m] == w, 1.0, 0.0)
                        term = weight * products[rank, k, :, pl.ds(p * tile, tile)]
                        total = term if total is None else total + term
                    parts.append(total)
                high, low = split(jnp.concatenate(parts, axis=0))
                halves.append(jnp.concatenate([high, high, low], axis=0))
            right = jnp.concatenate(halves, axis=1)
            result = jnp.dot(lift_cat, right, preferred_element_type=jnp.float32)
            for t in range(2 * coarse):
                for q in range(2):
                    value = result[t * tile:(t + 1) * tile, q * tile:(q + 1) * tile]
                    if t < coarse:
                        own_ref[t, 2 * c + q] += value
                    else:
                        following[t - coarse, 2 * c + q] += value

            @pl.when((n == span - 1) & has_right)
            def _():
                next_copy(c).start()

        return carry

    lax.fori_loop(0, span, one_distance, 0)

    for step in range(1, span):
        table_copy(step).wait_send()
    a_copy(send_order[0]).wait_send()
    if gated:
        @pl.when(first_core)
        def _():
            for step in send_order[1:]:
                a_copy(step).wait_send()
    else:
        for step in send_order[1:]:
            a_copy(step).wait_send()

    @pl.when(has_right)
    def _():
        for copy in halo_copies(0):
            copy.wait_send()
        for c in range(chunks):
            next_copy(c).wait_send()

    @pl.when(has_left)
    def _():
        for copy in halo_copies(1):
            copy.wait_send()
        for c in range(chunks):
            next_copy(c).wait_recv()


def shards(a_tiles, a_cols, new_row, p_tiles, p_cols):
    rows, tile = a_tiles.shape[0], a_tiles.shape[2]
    gx, gy = lax.axis_size("gx"), lax.axis_size("gy")
    span = min(SPAN, gx)
    coarse = rows // 4
    band = jax.ShapeDtypeStruct((coarse, 4 * coarse, tile, tile), jnp.float32)
    band_in = pltpu.VMEM(band.shape, jnp.float32)
    dma = pltpu.SemaphoreType.DMA
    row_block = (span, CAP, A_TILES, tile, tile)
    operands = [
        pltpu.with_memory_space_constraint(value, pltpu.HBM)
        for value in (new_row, a_cols.T, p_cols.T, a_tiles, p_tiles)]
    own, arrived = pl.pallas_call(
        functools.partial(kernel, span, gx, gy),
        out_shape=[band_in, band_in],
        in_specs=[pl.BlockSpec(memory_space=pl.ANY)] * 5,
        out_specs=[pl.BlockSpec(memory_space=pltpu.VMEM)] * 2,
        scratch_shapes=[
            pltpu.SMEM((rows,), jnp.int32),
            pltpu.SMEM((A_TILES, rows), jnp.int32),
            pltpu.SMEM((P_TILES, rows), jnp.int32),
            pltpu.VMEM(a_tiles.shape, jnp.float32),
            pltpu.VMEM(p_tiles.shape, jnp.float32),
            pltpu.VMEM(row_block, jnp.float32),
            pltpu.VMEM(row_block, jnp.float32),
            pltpu.VMEM((2, rows, P_TILES, tile, tile), jnp.float32),
            pltpu.VMEM((3 * rows, 3 * tile, P_TILES * tile), jnp.bfloat16),
            pltpu.VMEM((rows, P_TILES, tile, tile), jnp.float32),
            pltpu.VMEM((CAP, A_TILES, tile, P_TILES * tile), jnp.float32),
            pltpu.VMEM((coarse, 4 * coarse, tile, tile), jnp.float32),
            pltpu.VMEM((rows, LANES), jnp.int32),
            pltpu.VMEM((span, rows, LANES), jnp.int32),
            pltpu.VMEM((3, rows, LANES), jnp.int32),
            pltpu.SMEM((span, rows, LANES), jnp.int32),
            pltpu.SMEM((3, rows, LANES), jnp.int32),
            dma((span,)), dma((span,)), dma((span,)), dma((span,)),
            dma((2,)), dma((2,)), dma((2,)), dma((2,)),
            dma((2 * coarse,)), dma((2 * coarse,)), dma((5,)),
            pltpu.SemaphoreType.REGULAR,
        ],
        compiler_params=pltpu.CompilerParams(
            collective_id=0, has_side_effects=True, vmem_limit_bytes=48 * 1024 * 1024),
        name="galerkin",
    )(*operands)
    pad = ((0, 0), (coarse, 0), (0, 0), (0, 0))
    behind = ((0, 0), (0, coarse), (0, 0), (0, 0))
    return jnp.pad(own, pad) + jnp.pad(arrived, behind)


def solution(mesh):
    in_specs = (
        P(("gx", "gy"), None, None, None),
        P(("gx", "gy"), None),
        P(("gx", "gy")),
        P(("gx", "gy"), None, None, None),
        P(("gx", "gy"), None),
    )
    out_specs = P(("gx", "gy"), None, None, None)
    return jax.shard_map(shards, mesh=mesh, in_specs=in_specs, out_specs=out_specs, check_vma=False)
```

```python
import functools

import jax
import jax.numpy as jnp
from jax import lax
from jax.experimental import pallas as pl
from jax.experimental.pallas import tpu as pltpu
from jax.sharding import PartitionSpec as P

A_TILES = 4
P_TILES = 2
CAP = 2
SPAN = 6
LANES = 128
ROW_LANE = A_TILES
P_LANE = A_TILES + 1


def split(value):
    high = value.astype(jnp.bfloat16)
    low = (value - high.astype(jnp.float32)).astype(jnp.bfloat16)
    return high, low


def find_row(new_row_of, rows, per_owner, owner, rank):
    seen = jnp.int32(0)
    found = jnp.int32(0)
    for row in range(rows):
        here = lax.div(new_row_of(row), jnp.int32(per_owner)) == owner
        found = jnp.where(here & (seen == rank), row, found)
        seen = seen + here.astype(jnp.int32)
    return found, seen > rank


def may_reach(k, p, place):
    columns = (1,) if k == 0 else (0, 1, 2)
    if p == 0:
        return place in columns
    return place - 1 in columns or place == 1


def kernel(
    span, gx, gy,
    new_row_hbm, a_cols_hbm, p_cols_hbm, a_hbm, p_hbm,
    own_ref, arrived_ref,
    new_row_ref, a_cols_ref, p_cols_ref, a_ref, p_ref,
    stage, recv, ext, ext_cat, flipped, products, following,
    table, table_from, table_ext, from_s, ext_s,
    a_send, a_recv, t_send, t_recv, h_send, h_recv, ht_send, ht_recv, n_send, n_recv, local_sem, gate,
):
    rows, tile = p_ref.shape[0], p_ref.shape[2]
    coarse = rows // 4
    chunks = 4 * coarse // 2
    x, y = lax.axis_index("gx"), lax.axis_index("gy")
    device = x * gy + y
    per_owner = rows * gy
    has_left, has_right = y > 0, y < gy - 1
    gated = gx == 4 and span == 4 and gy % 2 == 0
    first_core = lax.rem(y, 2) == 0

    inputs = [
        pltpu.make_async_copy(source, target, local_sem.at[n])
        for n, (source, target) in enumerate((
            (a_hbm, a_ref), (new_row_hbm, new_row_ref), (a_cols_hbm, a_cols_ref),
            (p_cols_hbm, p_cols_ref), (p_hbm, p_ref)))]
    for copy in inputs:
        copy.start()

    barrier = pltpu.get_barrier_semaphore()
    for step in range(1, span):
        pl.semaphore_signal(
            barrier, inc=1, device_id={"gx": lax.rem(x + gx - step, gx)},
            device_id_type=pl.DeviceIdType.MESH)

    @pl.when(has_left)
    def _():
        pl.semaphore_signal(
            barrier, inc=1, device_id={"gy": y - 1}, device_id_type=pl.DeviceIdType.MESH)

    @pl.when(has_right)
    def _():
        pl.semaphore_signal(
            barrier, inc=1, device_id={"gy": y + 1}, device_id_type=pl.DeviceIdType.MESH)

    for copy in inputs[1:4]:
        copy.wait()
    row_id = lax.broadcasted_iota(jnp.int32, (rows, LANES), 0)
    lane_id = lax.broadcasted_iota(jnp.int32, (rows, LANES), 1)
    filled = jnp.zeros((rows, LANES), jnp.int32)
    for row in range(rows):
        entries = [a_cols_ref[k, row] for k in range(A_TILES)]
        entries += [new_row_ref[row]]
        entries += [p_cols_ref[q, row] for q in range(P_TILES)]
        for lane, entry in enumerate(entries):
            filled = jnp.where((row_id == row) & (lane_id == lane), entry, filled)
    table[...] = filled
    table_from[0] = filled
    table_ext[1] = filled

    def put_rows(step, target, slot):
        owner = lax.rem(x + step, gx)
        for rank in range(CAP):
            row, _ = find_row(lambda r: new_row_ref[r], rows, per_owner, owner, rank)
            target[slot, rank] = a_ref[row]

    def a_copy(step):
        return pltpu.make_async_remote_copy(
            stage.at[step], recv.at[step], a_send.at[step], a_recv.at[step],
            device_id={"gx": lax.rem(x + step, gx)}, device_id_type=pl.DeviceIdType.MESH)

    def table_copy(step):
        return pltpu.make_async_remote_copy(
            table, table_from.at[step], t_send.at[step], t_recv.at[step],
            device_id={"gx": lax.rem(x + step, gx)}, device_id_type=pl.DeviceIdType.MESH)

    def halo_copies(side):
        target = y + 1 if side == 0 else y - 1
        place = 0 if side == 0 else 2
        return (
            pltpu.make_async_remote_copy(
                table, table_ext.at[place], ht_send.at[side], ht_recv.at[side],
                device_id={"gy": target}, device_id_type=pl.DeviceIdType.MESH),
            pltpu.make_async_remote_copy(
                p_hbm, ext.at[side], h_send.at[side], h_recv.at[side],
                device_id={"gy": target}, device_id_type=pl.DeviceIdType.MESH),
        )

    if gx == 4 and span == 4:
        odd = lax.rem(x, 2)
        send_order = [2, 3 - 2 * odd, 1 + 2 * odd]

        def arrival(n):
            later = n // 2
            return 2 * n * (1 - later) + later * (
                (1 - odd) * (3 - 2 * (n - 2)) + odd * (1 + 2 * (n - 2)))
    else:
        send_order = list(range(1, span))

        def arrival(n):
            return n

    inputs[0].wait()
    put_rows(send_order[0], stage, send_order[0])
    greeted = span - 1 + jnp.where(has_left, 1, 0) + jnp.where(has_right, 1, 0)
    pl.semaphore_wait(barrier, greeted)
    a_copy(send_order[0]).start()
    for step in range(1, span):
        table_copy(step).start()

    @pl.when(has_right)
    def _():
        for copy in halo_copies(0):
            copy.start()

    @pl.when(has_left)
    def _():
        for copy in halo_copies(1):
            copy.start()

    for n, step in enumerate(send_order[1:]):
        put_rows(step, stage, step)
        if gated and n == 0:
            @pl.when(jnp.logical_not(first_core))
            def _():
                a_copy(step).start()
        else:
            a_copy(step).start()
    put_rows(0, recv, 0)

    def split_p(source, base):
        def body(row, carry):
            for q in range(P_TILES):
                high, low = split(source[row, q])
                columns = pl.ds(q * tile, tile)
                ext_cat[base + row, pl.ds(0, tile), columns] = high
                ext_cat[base + row, pl.ds(tile, tile), columns] = high
                ext_cat[base + row, pl.ds(2 * tile, tile), columns] = low
            return carry
        lax.fori_loop(0, rows, body, 0)

    def flip(row, carry):
        for q in range(P_TILES):
            flipped[row, q] = p_ref[row, q].T
        return carry

    inputs[4].wait()
    lax.fori_loop(0, rows, flip, 0)
    split_p(p_ref, rows)

    def clear(n, carry):
        for t in range(coarse):
            own_ref[t, n] = jnp.zeros((tile, tile), jnp.float32)
            following[t, n] = jnp.zeros((tile, tile), jnp.float32)
        return carry

    lax.fori_loop(0, 4 * coarse, clear, 0)

    @pl.when(jnp.logical_not(has_left))
    def _():
        copy = pltpu.make_async_copy(following, arrived_ref, local_sem.at[0])
        copy.start()
        copy.wait()

    for step in range(1, span):
        table_copy(step).wait_recv()

    @pl.when(has_left)
    def _():
        for copy in halo_copies(0):
            copy.wait_recv()
        split_p(ext.at[0], 0)

    @pl.when(jnp.logical_not(has_left))
    def _():
        table_ext[0] = jnp.zeros((rows, LANES), jnp.int32)

    @pl.when(has_right)
    def _():
        for copy in halo_copies(1):
            copy.wait_recv()
        split_p(ext.at[1], 2 * rows)

    @pl.when(jnp.logical_not(has_right))
    def _():
        table_ext[2] = jnp.zeros((rows, LANES), jnp.int32)

    to_scalar = (
        pltpu.make_async_copy(table_from, from_s, local_sem.at[0]),
        pltpu.make_async_copy(table_ext, ext_s, local_sem.at[1]),
    )
    for copy in to_scalar:
        copy.start()
    for copy in to_scalar:
        copy.wait()

    def next_copy(n):
        piece = pl.ds(2 * n, 2)
        return pltpu.make_async_remote_copy(
            following.at[:, piece], arrived_ref.at[:, piece], n_send.at[n], n_recv.at[n],
            device_id={"gy": y + 1}, device_id_type=pl.DeviceIdType.MESH)

    def one_distance(n, carry):
        step = arrival(n)
        if gated:
            @pl.when((n == 1) & first_core)
            def _():
                pl.semaphore_wait(gate, 1)
                a_copy(send_order[1]).start()

            @pl.when((n == 2) & jnp.logical_not(first_core))
            def _():
                for sent in send_order[:2]:
                    a_copy(sent).wait_send()
                pl.semaphore_signal(
                    gate, inc=1, device_id={"gy": y - 1}, device_id_type=pl.DeviceIdType.MESH)

        @pl.when(n > 0)
        def _():
            a_copy(step).wait_recv()

        slots = []
        lifts = [[] for _ in range(2 * coarse)]
        for rank in range(CAP):
            row, there = find_row(
                lambda r: from_s[step, r, ROW_LANE], rows, per_owner, x, rank)
            own_row = lax.rem(from_s[step, row, ROW_LANE], jnp.int32(rows))
            wide = []
            for k in range(A_TILES):
                column = jnp.where(there, from_s[step, row, k] - (device - 1) * rows, rows)
                column = jnp.minimum(jnp.maximum(column, 0), 3 * rows - 1)
                for q in range(P_TILES):
                    goal = ext_s[lax.div(column, rows), lax.rem(column, rows), P_LANE + q]
                    wide.append(jnp.where(there, goal - (device - 1) * coarse, -1))
                high, low = split(recv[step, rank, k])
                left = jnp.concatenate([high, low, high], axis=1)
                products[rank, k] = jnp.dot(
                    left, ext_cat[column], preferred_element_type=jnp.float32)
            slots.append(wide)
            goals = [
                ext_s[1, own_row, P_LANE + p] - device * coarse for p in range(P_TILES)]
            for t in range(2 * coarse):
                lifts[t].append(sum(
                    jnp.where(goals[p] == t, 1.0, 0.0) * flipped[own_row, p]
                    for p in range(P_TILES)))
        lift_cat = []
        for t in range(2 * coarse):
            high, low = split(jnp.concatenate(lifts[t], axis=1))
            lift_cat.append(jnp.concatenate([high, low, high], axis=1))
        lift_cat = jnp.concatenate(lift_cat, axis=0)

        for c in range(chunks):
            halves = []
            for q in range(2):
                w = 2 * c + q
                parts = []
                for rank in range(CAP):
                    total = None
                    for m in range(A_TILES * P_TILES):
                        k, p = m // P_TILES, m % P_TILES
                        if not may_reach(k, p, w // coarse):
                            continue
                        weight = jnp.where(slots[rank][m] == w, 1.0, 0.0)
                        term = weight * products[rank, k, :, pl.ds(p * tile, tile)]
                        total = term if total is None else total + term
                    parts.append(total)
                high, low = split(jnp.concatenate(parts, axis=0))
                halves.append(jnp.concatenate([high, high, low], axis=0))
            right = jnp.concatenate(halves, axis=1)
            result = jnp.dot(lift_cat, right, preferred_element_type=jnp.float32)
            for t in range(2 * coarse):
                for q in range(2):
                    value = result[t * tile:(t + 1) * tile, q * tile:(q + 1) * tile]
                    if t < coarse:
                        own_ref[t, 2 * c + q] += value
                    else:
                        following[t - coarse, 2 * c + q] += value

            @pl.when((n == span - 1) & has_right)
            def _():
                next_copy(c).start()

        return carry

    lax.fori_loop(0, span, one_distance, 0)

    for step in range(1, span):
        table_copy(step).wait_send()
    if gated:
        @pl.when(first_core)
        def _():
            for step in send_order[:2]:
                a_copy(step).wait_send()

        a_copy(send_order[2]).wait_send()
    else:
        for step in send_order:
            a_copy(step).wait_send()

    @pl.when(has_right)
    def _():
        for copy in halo_copies(0):
            copy.wait_send()
        for c in range(chunks):
            next_copy(c).wait_send()

    @pl.when(has_left)
    def _():
        for copy in halo_copies(1):
            copy.wait_send()
        for c in range(chunks):
            next_copy(c).wait_recv()


def shards(a_tiles, a_cols, new_row, p_tiles, p_cols):
    rows, tile = a_tiles.shape[0], a_tiles.shape[2]
    gx, gy = lax.axis_size("gx"), lax.axis_size("gy")
    span = min(SPAN, gx)
    coarse = rows // 4
    band = jax.ShapeDtypeStruct((coarse, 4 * coarse, tile, tile), jnp.float32)
    band_in = pltpu.VMEM(band.shape, jnp.float32)
    dma = pltpu.SemaphoreType.DMA
    row_block = (span, CAP, A_TILES, tile, tile)
    operands = [
        pltpu.with_memory_space_constraint(value, pltpu.HBM)
        for value in (new_row, a_cols.T, p_cols.T, a_tiles, p_tiles)]
    own, arrived = pl.pallas_call(
        functools.partial(kernel, span, gx, gy),
        out_shape=[band_in, band_in],
        in_specs=[pl.BlockSpec(memory_space=pl.ANY)] * 5,
        out_specs=[pl.BlockSpec(memory_space=pltpu.VMEM)] * 2,
        scratch_shapes=[
            pltpu.SMEM((rows,), jnp.int32),
            pltpu.SMEM((A_TILES, rows), jnp.int32),
            pltpu.SMEM((P_TILES, rows), jnp.int32),
            pltpu.VMEM(a_tiles.shape, jnp.float32),
            pltpu.VMEM(p_tiles.shape, jnp.float32),
            pltpu.VMEM(row_block, jnp.float32),
            pltpu.VMEM(row_block, jnp.float32),
            pltpu.VMEM((2, rows, P_TILES, tile, tile), jnp.float32),
            pltpu.VMEM((3 * rows, 3 * tile, P_TILES * tile), jnp.bfloat16),
            pltpu.VMEM((rows, P_TILES, tile, tile), jnp.float32),
            pltpu.VMEM((CAP, A_TILES, tile, P_TILES * tile), jnp.float32),
            pltpu.VMEM((coarse, 4 * coarse, tile, tile), jnp.float32),
            pltpu.VMEM((rows, LANES), jnp.int32),
            pltpu.VMEM((span, rows, LANES), jnp.int32),
            pltpu.VMEM((3, rows, LANES), jnp.int32),
            pltpu.SMEM((span, rows, LANES), jnp.int32),
            pltpu.SMEM((3, rows, LANES), jnp.int32),
            dma((span,)), dma((span,)), dma((span,)), dma((span,)),
            dma((2,)), dma((2,)), dma((2,)), dma((2,)),
            dma((2 * coarse,)), dma((2 * coarse,)), dma((5,)),
            pltpu.SemaphoreType.REGULAR,
        ],
        compiler_params=pltpu.CompilerParams(
            collective_id=0, has_side_effects=True, vmem_limit_bytes=48 * 1024 * 1024),
        name="galerkin",
    )(*operands)
    pad = ((0, 0), (coarse, 0), (0, 0), (0, 0))
    behind = ((0, 0), (0, coarse), (0, 0), (0, 0))
    return jnp.pad(own, pad) + jnp.pad(arrived, behind)


def solution(mesh):
    in_specs = (
        P(("gx", "gy"), None, None, None),
        P(("gx", "gy"), None),
        P(("gx", "gy")),
        P(("gx", "gy"), None, None, None),
        P(("gx", "gy"), None),
    )
    out_specs = P(("gx", "gy"), None, None, None)
    return jax.shard_map(shards, mesh=mesh, in_specs=in_specs, out_specs=out_specs, check_vma=False)
```
